512 devices in a mesh: section: 32 (over x, z_lo), fsdp: 16 (over y, z_hi, core).
Axes of the slice: x: 4, y: 4, z: 16 (z_hi: 2, z_lo: 8; z = z_hi * 8 + z_lo), core: 2. Of those that a mesh axis runs over, the one named last changes fastest.
Arguments:
- table: bfloat16 [128000, 3584], P(('section', 'fsdp')), may hold values from -6 to 6
- hidden_states: bfloat16 [128, 3584], P('fsdp', 'section'), may hold values from -52 to 52
- embed_cotangent: bfloat16 [128, 3584], P('fsdp', 'section'), may hold values from -6 to 6
- teacher_logits: bfloat16 [128000, 128], P(('section', 'fsdp')), may hold values from -28 to 216
- student_ids: int32 [128], replicated, may hold values from 0 to 127999
- loss_mask: int32 [128], replicated, may hold values 0 or 1
Outputs:
- table_grad: bfloat16 [128000, 3584], P(('section', 'fsdp'))
- state_grad: bfloat16 [128, 3584], P('fsdp', 'section')
- loss: float32 [], replicated
The draws below stay inside these ranges and needn't reach their ends.
All inputs are finite; a program needn't handle non-finite values.
Results may differ from the reference program's by a relative error of at most 0.014.
Values may be sent and summed in bfloat16 or wider, within the bound.
A program may use at most 64 MiB of HBM per device.

```python
import math
import jax
import jax.numpy as jnp
from jax import lax

D = 3584
VOC_DEV = 250
TOKENS = 128
VOC = 128000


def draw_table(key, part):
    key = jax.random.fold_in(key, 11)
    values = jax.random.truncated_normal(key, -6.0, 6.0, (VOC, D), jnp.float32)
    values = values * (2.0 / math.sqrt(D))
    return values.astype(jnp.bfloat16)


def draw_hidden_states(key, part):
    key = jax.random.fold_in(key, 23)
    first = jax.random.fold_in(key, 0)
    values = jax.random.truncated_normal(first, -6.0, 6.0, (TOKENS, D), jnp.float32)
    return values.astype(jnp.bfloat16)


def draw_embed_cotangent(key, part):
    key = jax.random.fold_in(key, 41)
    scale = 256.0 / (VOC * math.sqrt(TOKENS))
    values = jax.random.truncated_normal(key, -6.0, 6.0, (TOKENS, D), jnp.float32)
    return (values * scale).astype(jnp.bfloat16)


def draw_teacher_logits(key, part):
    key = jax.random.fold_in(key, 37)
    first, second = jax.random.split(key, 2)
    home = jax.random.randint(second, (1, TOKENS), 0, VOC // VOC_DEV)
    block_of = jax.lax.broadcasted_iota(jnp.int32, (VOC, TOKENS), 0) // VOC_DEV
    boost = jnp.where(block_of == home, 8.0, 0.0)
    values = 4.0 * jax.random.truncated_normal(first, -6.0, 6.0, (VOC, TOKENS), jnp.float32) + boost
    return values.astype(jnp.bfloat16)


def set_ends(array, own_key, smallest, high):
    longest = array.shape.index(max(array.shape))
    spots = []
    for shift in (0, 1):
        where = [jax.random.randint(jax.random.fold_in(own_key, axis), (), 0, length) for axis, length in enumerate(array.shape)]
        where[longest] = (where[longest] + shift) % array.shape[longest]
        spots.append(tuple(where))
    return array.at[spots[0]].set(smallest).at[spots[1]].set(high)


def setup_inputs(seed: int = 0) -> dict:
    seeds = jax.random.split(jax.random.key(seed), 7)
    return {
        "table": draw_table(jax.random.fold_in(seeds[6], 71), 0),
        "hidden_states": draw_hidden_states(jax.random.fold_in(seeds[6], 71), 0),
        "embed_cotangent": draw_embed_cotangent(jax.random.fold_in(seeds[6], 71), 0),
        "teacher_logits": draw_teacher_logits(jax.random.fold_in(seeds[6], 71), 0),
        "student_ids": set_ends(jax.random.randint(seeds[4], (TOKENS,), 0, VOC), jax.random.fold_in(seeds[4], 1), 0, VOC - 1).astype(jnp.int32),
        "loss_mask": set_ends((jax.random.randint(seeds[5], (TOKENS,), 0, 4) < 3).astype(jnp.int32), jax.random.fold_in(seeds[5], 1), 0, 1),
    }


CONTRACT_LAST = (((1,), (1,)), ((), ()))
CONTRACT_FIRST = (((0,), (0,)), ((), ()))


def reference(table, hidden_states, embed_cotangent, teacher_logits, student_ids, loss_mask):
    logits = lax.dot_general(table, hidden_states, CONTRACT_LAST, preferred_element_type=jnp.float32)
    teach = teacher_logits.astype(jnp.float32)
    peak_s = jnp.max(logits, axis=0)
    peak_t = jnp.max(teach, axis=0)
    student_exp = jnp.exp(logits - peak_s[None, :])
    sum_s = jnp.sum(student_exp, axis=0)
    cross = jnp.sum(student_exp * (logits - teach), axis=0)
    sum_t = jnp.sum(jnp.exp(teach - peak_t[None, :]), axis=0)
    vocab_ids = lax.broadcasted_iota(jnp.int32, logits.shape, 0)
    log_zs = peak_s + jnp.log(sum_s)
    log_zt = peak_t + jnp.log(sum_t)
    kl_term = cross / sum_s - log_zs + log_zt
    weight = loss_mask.astype(jnp.float32) / TOKENS
    loss = jnp.sum(weight * kl_term)
    prob = jnp.exp(logits - log_zs[None, :])
    inner = prob * (logits - teach - log_zs[None, :] + log_zt[None, :] - kl_term[None, :])
    grad_logits = (weight[None, :] * inner).astype(jnp.bfloat16)
    state_grad = lax.dot_general(grad_logits, table, CONTRACT_FIRST, preferred_element_type=jnp.float32).astype(jnp.bfloat16)
    blocks = VOC // VOC_DEV
    selector = (vocab_ids == student_ids[None, :].astype(jnp.int32)).astype(jnp.bfloat16)
    grad_blocks = grad_logits.reshape(blocks, VOC_DEV, TOKENS)
    select_blocks = selector.reshape(blocks, VOC_DEV, TOKENS)

    def one_block(pair):
        block_grad, block_select = pair
        total = jnp.dot(block_grad, hidden_states, preferred_element_type=jnp.float32)
        total = total + jnp.dot(block_select, embed_cotangent, preferred_element_type=jnp.float32)
        return total.astype(jnp.bfloat16)

    table_grad = lax.map(one_block, (grad_blocks, select_blocks)).reshape(VOC, D)
    return table_grad, state_grad, loss
```

```python
import functools

import jax
import jax.numpy as jnp
from jax import lax
from jax.experimental import pallas as pl
from jax.experimental.pallas import tpu as pltpu
from jax.sharding import PartitionSpec as P

MESH = pl.DeviceIdType.MESH
F32, BF16 = jnp.float32, jnp.bfloat16
CONTRACT_LAST = (((1,), (1,)), ((), ()))
CONTRACT_FIRST = (((0,), (0,)), ((), ()))
NX, NY, NLO, NHI, NCORE = 4, 4, 8, 2, 2
NZ = NLO * NHI
NXY = NX * NY


def merge(maxes, *sums):
    top = jnp.max(maxes, axis=0, keepdims=True)
    scale = jnp.exp(maxes - top)
    return (top, *(jnp.sum(s * scale, axis=0, keepdims=True) for s in sums))


def merge_tiles(ref):
    peak_s, sum_s, cross = merge(ref[:, 0, :], ref[:, 1, :], ref[:, 2, :])
    peak_t, sum_t = merge(ref[:, 3, :], ref[:, 4, :])
    return peak_s, sum_s, cross, peak_t, sum_t


def tile_of(rows):
    return jnp.concatenate([*rows, jnp.zeros((3, rows[0].shape[1]), F32)], axis=0)


def kernel(
    table_hbm, hidden_ref, cot_ref, teach_hbm, ids_ref, mask_ref,
    grad_hbm, state_ref, loss_ref,
    table, teach_in, pack, first, lanes, hc, stat_core, stat_z, stat_xy,
    logits_ref, glog_ref, own_part, out_part, sib_part, t_ref, u_ref, v_ref, w_ref, z_src, z_dst, grad_ref,
    load_sem, store_sem, ag1_send, ag1_recv, ag2_send, ag2_recv, ag3_send, ag3_recv, sib_send, sib_recv,
    st_send, st_recv, rs0_send, rs0_recv, rs1_send, rs1_recv, rs2_send, rs2_recv, rs3_send, rs3_recv,
):
    section, fsdp = lax.axis_index("section"), lax.axis_index("fsdp")
    x, lo = section // NLO, lax.rem(section, NLO)
    y, hi, core = fsdp // (NHI * NCORE), lax.rem(fsdp // NCORE, NHI), lax.rem(fsdp, NCORE)
    z = hi * NLO + lo
    other = 1 - core
    a, b = x + core * (y - x), y + core * (x - y)

    def device(x_, y_, z_, core_):
        return (x_ * NLO + lax.rem(z_, NLO), y_ * (NHI * NCORE) + (z_ // NLO) * NCORE + core_)

    def xy(a_, b_):
        return a_ + core * (b_ - a_), b_ + core * (a_ - b_)

    def send(src, dst, send_sem, recv_sem, target):
        pltpu.make_async_remote_copy(
            src_ref=src, dst_ref=dst, send_sem=send_sem, recv_sem=recv_sem, device_id=target, device_id_type=MESH
        ).start()

    def arrive(ref, sem):
        pltpu.make_async_copy(ref, ref, sem).wait()

    loads = [
        pltpu.make_async_copy(table_hbm, table, load_sem.at[0]),
        pltpu.make_async_copy(teach_hbm, teach_in, load_sem.at[1]),
    ]
    for load in loads:
        load.start()

    barrier = pltpu.get_barrier_semaphore()

    def greet_z(j, carry):
        z_ = lax.rem(z + j, NZ)
        pl.semaphore_signal(barrier, inc=1, device_id=device(x, y, z_, core), device_id_type=MESH)
        pl.semaphore_signal(barrier, inc=1, device_id=device(x, y, z_, other), device_id_type=MESH)
        return carry

    def greet_xy(j, carry):
        p = lax.rem(x * NY + y + j, NXY)
        pl.semaphore_signal(barrier, inc=1, device_id=device(p // NY, lax.rem(p, NY), z, core), device_id_type=MESH)
        return carry

    pl.semaphore_signal(barrier, inc=1, device_id=device(x, y, z, other), device_id_type=MESH)
    lax.fori_loop(1, NZ, greet_z, 0)
    lax.fori_loop(1, NXY, greet_xy, 0)

    pack[...] = jnp.zeros_like(pack)
    pack[:, 0:112] = jnp.concatenate([hidden_ref[...].astype(F32), cot_ref[...].astype(F32)], axis=0).astype(BF16)
    pl.semaphore_wait(barrier, 1 + 2 * (NZ - 1) + NXY - 1)

    def gather_z(j, carry):
        send(pack, first.at[lo, core], ag1_send, ag1_recv, device(x, y, lax.rem(z + j, NZ), hi))
        return carry

    lax.fori_loop(1, NZ, gather_z, 0)

    @pl.when(core == hi)
    def _():
        pltpu.make_async_copy(pack, first.at[lo, core], ag1_recv).start()

    @pl.when(core != hi)
    def _():
        send(pack, first.at[lo, core], ag1_send, ag1_recv, device(x, y, z, hi))

    loads[1].wait()
    teach = teach_in[...].astype(F32)
    top_t = jnp.max(teach, axis=0, keepdims=True)
    total_t = jnp.sum(jnp.exp(teach - top_t), axis=0, keepdims=True)

    arrive(first, ag1_recv)
    for j in range(NLO):
        left, right = first[j, 0].astype(F32), first[j, 1].astype(F32)
        for t in range(2):
            rows = jnp.concatenate([left[8 * t : 8 * t + 8], right[8 * t : 8 * t + 8]], axis=0)
            lanes[t, :, 112 * j : 112 * (j + 1)] = rows[:, 0:112]
    for t in range(2):
        hc[x, t, y, core] = lanes[t].astype(BF16)
        for j in range(1, 4):
            block = hc.at[x, t, y, core]
            send(block, block, ag2_send.at[t], ag2_recv.at[t], device(*xy(a, lax.rem(b + j, 4)), z, core))

    def to_sibling(t, a_):
        for i in range(4):
            xi, yi = xy(a_, i)
            block = hc.at[xi, t, yi, core]
            send(block, block, sib_send.at[t], sib_recv.at[t], device(x, y, z, other))

    def gather_last(t):
        for j in range(1, 4):
            target = device(*xy(lax.rem(a + j, 4), b), z, core)
            for i in range(4):
                xi, yi = xy(a, i)
                block = hc.at[xi, t, yi, core]
                send(block, block, ag3_send.at[t], ag3_recv.at[t], target)

    three = hc.at[0:3, 0, 0, 0]
    twelve = hc.at[0:3, 0, 0:2]
    sixteen = hc.at[0]

    arrive(three, ag2_recv.at[0])
    gather_last(0)
    to_sibling(0, a)
    arrive(three, ag2_recv.at[1])
    to_sibling(1, a)
    loads[0].wait()
    arrive(twelve, ag3_recv.at[0])
    for j in range(1, 4):
        to_sibling(0, lax.rem(a + j, 4))
    gather_last(1)
    arrive(sixteen, sib_recv.at[0])

    total = None
    for c in range(NX):
        states = hc[c, 0].reshape(128, 896)
        term = lax.dot_general(table[:, 896 * c : 896 * (c + 1)], states, CONTRACT_LAST, preferred_element_type=F32)
        total = term if total is None else total + term
    logits_ref[...] = total
    peak = jnp.max(total, axis=0, keepdims=True)
    weights = jnp.exp(total - peak)
    stat_core[core] = tile_of(
        [
            peak,
            jnp.sum(weights, axis=0, keepdims=True),
            jnp.sum(weights * (total - teach), axis=0, keepdims=True),
            top_t,
            total_t,
        ]
    )
    send(stat_core.at[core], stat_core.at[core], st_send.at[0], st_recv.at[0], device(x, y, z, other))
    arrive(stat_core.at[0], st_recv.at[0])
    stat_z[z] = tile_of(merge_tiles(stat_core))

    def share_z(j, carry):
        send(stat_z.at[z], stat_z.at[z], st_send.at[1], st_recv.at[1], device(x, y, lax.rem(z + j, NZ), core))
        return carry

    lax.fori_loop(1, NZ, share_z, 0)
    arrive(twelve, ag3_recv.at[1])
    for j in range(1, 4):
        to_sibling(1, lax.rem(a + j, 4))
    arrive(stat_z.at[0 : NZ - 1], st_recv.at[1])
    me = x * NY + y
    stat_xy[me] = tile_of(merge_tiles(stat_z))

    def share_xy(j, carry):
        p = lax.rem(me + j, NXY)
        send(stat_xy.at[me], stat_xy.at[me], st_send.at[2], st_recv.at[2], device(p // NY, lax.rem(p, NY), z, core))
        return carry

    lax.fori_loop(1, NXY, share_xy, 0)
    arrive(stat_xy.at[0 : NXY - 1], st_recv.at[2])
    peak_s, sum_s, cross, peak_t, sum_t = merge_tiles(stat_xy)

    log_zs = peak_s + jnp.log(sum_s)
    log_zt = peak_t + jnp.log(sum_t)
    kl_term = cross / sum_s - log_zs + log_zt
    weight = mask_ref[...].astype(F32) / 128.0
    loss_ref[...] = jnp.broadcast_to(jnp.sum(weight * kl_term, axis=1, keepdims=True), loss_ref.shape)
    logits = logits_ref[...]
    prob = jnp.exp(logits - log_zs)
    inner = prob * (logits - teach_in[...].astype(F32) - log_zs + log_zt - kl_term)
    glog = (weight * inner).astype(BF16)
    glog_ref[...] = glog

    for c in range(NX):
        part = lax.dot_general(glog, table[:, 896 * c : 896 * (c + 1)], CONTRACT_FIRST, preferred_element_type=F32)
        part = part.reshape(NY, NHI, 16, 896)
        own_part[c] = part
        out_part[c] = part.astype(BF16)
        send(out_part.at[c, :, other], sib_part.at[c], rs0_send.at[c], rs0_recv.at[c], device(x, y, z, other))
    for c in range(NX):
        arrive(sib_part.at[c], rs0_recv.at[c])
        for r in range(NY):
            ai, bi = xy(c, r)
            t_ref[ai, bi] = (own_part[c, r, core] + sib_part[c, r].astype(F32)).astype(BF16)
    for j in range(1, 4):
        a_ = lax.rem(a + j, 4)
        send(t_ref.at[a_], u_ref.at[a], rs1_send, rs1_recv, device(*xy(a_, b), z, core))

    arrive(sixteen, sib_recv.at[1])
    rows = glog_ref.shape[0]
    entries = (section * (NY * NHI * NCORE) + fsdp) * rows + lax.broadcasted_iota(jnp.int32, (rows, 128), 0)
    selector = (entries == ids_ref[...]).astype(BF16)
    both = jnp.concatenate([glog_ref[...], selector], axis=1)
    for c in range(NX):
        grad_ref[:, 896 * c : 896 * (c + 1)] = jnp.dot(
            both, hc[c].reshape(256, 896), preferred_element_type=F32
        ).astype(BF16)
    store = pltpu.make_async_copy(grad_ref, grad_hbm, store_sem)
    store.start()

    arrive(u_ref.at[0:3], rs1_recv)
    for r in range(4):
        acc = t_ref[a, r].astype(F32)
        for j in range(1, 4):
            acc = acc + u_ref[lax.rem(a + j, 4), r].astype(F32)
        v_ref[r] = acc.astype(BF16)
    for j in range(1, 4):
        b_ = lax.rem(b + j, 4)
        send(v_ref.at[b_], w_ref.at[b], rs2_send, rs2_recv, device(*xy(a, b_), z, core))
    arrive(w_ref.at[0:3], rs2_recv)
    acc = v_ref[b].astype(F32)
    for j in range(1, 4):
        acc = acc + w_ref[lax.rem(b + j, 4)].astype(F32)
    lanes[0] = acc
    z_src[...] = jnp.zeros_like(z_src)
    for j in range(NLO):
        for k in range(NCORE):
            z_src[j, k, :, 0:112] = lanes[0, 8 * k : 8 * k + 8, 112 * j : 112 * (j + 1)]

    def reduce_z(j, carry):
        lo_ = lax.rem(lo + j, NLO)
        for k in range(NCORE):
            send(z_src.at[lo_, k], z_dst.at[z], rs3_send, rs3_recv, device(x, y, core * NLO + lo_, k))
        return carry

    lax.fori_loop(1, NLO, reduce_z, 0)
    send(z_src.at[lo, other], z_dst.at[z], rs3_send, rs3_recv, device(x, y, core * NLO + lo, other))

    @pl.when(core == hi)
    def _():
        pltpu.make_async_copy(z_src.at[lo, core], z_dst.at[z], rs3_recv).start()

    @pl.when(core != hi)
    def _():
        send(z_src.at[lo, core], z_dst.at[z], rs3_send, rs3_recv, device(x, y, core * NLO + lo, core))

    arrive(z_dst, rs3_recv)
    state_ref[...] = jnp.sum(z_dst[...], axis=0)[:, 0:112].astype(BF16)

    tiles = first.reshape(NZ, 16, 128)

    @pl.when(core == hi)
    def _():
        arrive(tiles.at[0 : NZ - 1], ag1_send)
        arrive(z_dst.at[0 : NZ - 1], rs3_send)

    @pl.when(core != hi)
    def _():
        arrive(tiles, ag1_send)
        arrive(z_dst, rs3_send)

    for t in range(2):
        arrive(three, ag2_send.at[t])
        arrive(twelve, ag3_send.at[t])
        arrive(sixteen, sib_send.at[t])
    arrive(stat_core.at[0], st_send.at[0])
    arrive(stat_z.at[0 : NZ - 1], st_send.at[1])
    arrive(stat_xy.at[0 : NXY - 1], st_send.at[2])
    for c in range(NX):
        arrive(sib_part.at[c], rs0_send.at[c])
    arrive(u_ref.at[0:3], rs1_send)
    arrive(w_ref.at[0:3], rs2_send)
    store.wait()


def shards(table, hidden_states, embed_cotangent, teacher_logits, student_ids, loss_mask):
    rows, width = table.shape
    tokens = teacher_logits.shape[1]
    vmem = pl.BlockSpec(memory_space=pltpu.VMEM)
    hbm = pl.BlockSpec(memory_space=pl.ANY)
    dma = pltpu.SemaphoreType.DMA
    table_grad, state_grad, loss = pl.pallas_call(
        kernel,
        out_shape=(
            jax.ShapeDtypeStruct((rows, width), BF16),
            jax.ShapeDtypeStruct(hidden_states.shape, BF16),
            jax.ShapeDtypeStruct((1, 128), F32),
        ),
        in_specs=[hbm, vmem, vmem, hbm, vmem, vmem],
        out_specs=(hbm, vmem, vmem),
        scratch_shapes=[
            pltpu.VMEM((rows, width), BF16),
            pltpu.VMEM((rows, tokens), BF16),
            pltpu.VMEM((16, 128), BF16),
            pltpu.VMEM((NLO, NCORE, 16, 128), BF16),
            pltpu.VMEM((2, 16, 896), F32),
            pltpu.VMEM((NX, 2, NY, NHI, 16, 896), BF16),
            pltpu.VMEM((NCORE, 8, 128), F32),
            pltpu.VMEM((NZ, 8, 128), F32),
            pltpu.VMEM((NXY, 8, 128), F32),
            pltpu.VMEM((rows, tokens), F32),
            pltpu.VMEM((rows, tokens), BF16),
            pltpu.VMEM((NX, NY, NHI, 16, 896), F32),
            pltpu.VMEM((NX, NY, NHI, 16, 896), BF16),
            pltpu.VMEM((NX, NY, 16, 896), BF16),
            pltpu.VMEM((4, 4, 16, 896), BF16),
            pltpu.VMEM((4, 4, 16, 896), BF16),
            pltpu.VMEM((4, 16, 896), BF16),
            pltpu.VMEM((4, 16, 896), BF16),
            pltpu.VMEM((NLO, NCORE, 8, 128), F32),
            pltpu.VMEM((NZ, 8, 128), F32),
            pltpu.VMEM((rows, width), BF16),
            dma((2,)),
            dma,
            dma,
            dma,
            dma((2,)),
            dma((2,)),
            dma((2,)),
            dma((2,)),
            dma((2,)),
            dma((2,)),
            dma((3,)),
            dma((3,)),
            dma((4,)),
            dma((4,)),
            dma,
            dma,
            dma,
            dma,
            dma,
            dma,
        ],
        compiler_params=pltpu.CompilerParams(
            collective_id=0, has_side_effects=True, vmem_limit_bytes=40 * 1024 * 1024
        ),
    )(
        table,
        hidden_states,
        embed_cotangent,
        teacher_logits,
        student_ids.reshape(1, 128),
        loss_mask.reshape(1, 128),
    )
    return table_grad, state_grad, loss[0, 0]


def solution(mesh):
    return jax.shard_map(
        shards,
        mesh=mesh,
        in_specs=(
            P(("section", "fsdp"), None),
            P("fsdp", "section"),
            P("fsdp", "section"),
            P(("section", "fsdp"), None),
            P(),
            P(),
        ),
        out_specs=(P(("section", "fsdp"), None), P("fsdp", "section"), P()),
        check_vma=False,
    )
```

```python
import functools

import jax
import jax.numpy as jnp
from jax import lax
from jax.experimental import pallas as pl
from jax.experimental.pallas import tpu as pltpu
from jax.sharding import PartitionSpec as P

MESH = pl.DeviceIdType.MESH
F32, BF16 = jnp.float32, jnp.bfloat16
CONTRACT_LAST = (((1,), (1,)), ((), ()))
CONTRACT_FIRST = (((0,), (0,)), ((), ()))
NX, NY, NLO, NHI, NCORE = 4, 4, 8, 2, 2
NZ = NLO * NHI
NXY = NX * NY
VMEM_MIB = 60
FAR_Z = sorted(range(1, NZ), key=lambda j: -min(j, NZ - j))
FAR_XY = sorted(
    ((i, j) for i in range(NX) for j in range(NY) if i or j), key=lambda d: -sum(min(v, 4 - v) for v in d)
)


def merge(maxes, *sums):
    top = jnp.max(maxes, axis=0, keepdims=True)
    scale = jnp.exp(maxes - top)
    return (top, *(jnp.sum(s * scale, axis=0, keepdims=True) for s in sums))


def merge_tiles(ref):
    peak_s, sum_s, cross = merge(ref[:, 0, :], ref[:, 1, :], ref[:, 2, :])
    peak_t, sum_t = merge(ref[:, 3, :], ref[:, 4, :])
    return peak_s, sum_s, cross, peak_t, sum_t


def tile_of(rows):
    return jnp.concatenate([*rows, jnp.zeros((3, rows[0].shape[1]), F32)], axis=0)


class Copies:
    def __init__(self):
        self.arrivals, self.departures = {}, {}

    @staticmethod
    def wait(ref, sem):
        pltpu.make_async_copy(ref, ref, sem).wait()

    @staticmethod
    def send(src, dst, sems, target):
        pltpu.make_async_remote_copy(
            src_ref=src, dst_ref=dst, send_sem=sems[0], recv_sem=sems[1], device_id=target, device_id_type=MESH
        ).start()

    def expect(self, key, ref, sems):
        self.arrivals[key] = (ref, sems[1])
        self.departures[key] = (ref, sems[0])

    def arrive(self, key):
        self.wait(*self.arrivals.pop(key))

    def finish(self):
        for key in list(self.arrivals):
            self.arrive(key)
        for ref, sem in self.departures.values():
            self.wait(ref, sem)


def kernel(
    table_hbm, hidden_hbm, cot_hbm, teach_hbm, ids_hbm, mask_hbm,
    grad_hbm, state_ref, loss_ref,
    table, hidden_in, cot_in, teach_in, ids_in, mask_in,
    pack, first, lanes, hc, stat_core, stat_xy, stat_z,
    logits_ref, part, sib_part, t_ref, u_ref, cols_ref, z_src, z_dst, grad_ref,
    load_sem, store_sem, ag1_sem, plane_send, plane_recv, sib_sem, st_sem, rs0_sem, rs1_sem, rs2_sem,
):
    section, fsdp = lax.axis_index("section"), lax.axis_index("fsdp")
    x, lo = section // NLO, lax.rem(section, NLO)
    y, hi, core = fsdp // (NHI * NCORE), lax.rem(fsdp // NCORE, NHI), lax.rem(fsdp, NCORE)
    z, me = hi * NLO + lo, x * NY + y
    other = 1 - core

    def device(x_, y_, z_, core_):
        return (x_ * NLO + lax.rem(z_, NLO), y_ * (NHI * NCORE) + (z_ // NLO) * NCORE + core_)

    sibling = device(x, y, z, other)
    along_z = [lax.rem(z + j, NZ) for j in FAR_Z]
    in_plane = [(lax.rem(x + i, NX), lax.rem(y + j, NY)) for i, j in FAR_XY]
    copies = Copies()
    send = copies.send

    def pair(ref, *at):
        return ref.at[(0, *at)], ref.at[(1, *at)]

    loads = [
        pltpu.make_async_copy(src, dst, load_sem.at[i])
        for i, (src, dst) in enumerate(
            [
                (hidden_hbm, hidden_in), (cot_hbm, cot_in), (teach_hbm, teach_in),
                (table_hbm, table), (ids_hbm, ids_in), (mask_hbm, mask_in),
            ]
        )
    ]
    loads[0].start()
    loads[1].start()

    barrier = pltpu.get_barrier_semaphore()
    for z_ in along_z:
        pl.semaphore_signal(barrier, inc=1, device_id=device(x, y, z_, core), device_id_type=MESH)
        pl.semaphore_signal(barrier, inc=1, device_id=device(x, y, z_, other), device_id_type=MESH)
    for x_, y_ in in_plane:
        pl.semaphore_signal(barrier, inc=1, device_id=device(x_, y_, z, core), device_id_type=MESH)
    pl.semaphore_signal(barrier, inc=1, device_id=sibling, device_id_type=MESH)
    for load in loads[2:]:
        load.start()

    loads[0].wait()
    loads[1].wait()
    pack[...] = jnp.zeros_like(pack)
    pack[:, 0:112] = jnp.concatenate([hidden_in[...].astype(F32), cot_in[...].astype(F32)], axis=0).astype(BF16)
    pl.semaphore_wait(barrier, 1 + 2 * (NZ - 1) + NXY - 1)

    waited = [0, 1]
    tiles = first.reshape(NZ, 16, 128)
    gathers, stores = [], []

    def finish():
        for i, load in enumerate(loads):
            if i not in waited:
                load.wait()
        for sem, ref, less in gathers:

            @pl.when(core == hi)
            def _():
                copies.wait(less, sem)

            @pl.when(core != hi)
            def _():
                copies.wait(ref, sem)

        copies.finish()
        for store in stores:
            store.wait()


    sems = pair(ag1_sem)
    for z_ in along_z:
        send(pack, first.at[lo, core], sems, device(x, y, z_, hi))

    @pl.when(core == hi)
    def _():
        pltpu.make_async_copy(pack, first.at[lo, core], sems[1]).start()

    @pl.when(core != hi)
    def _():
        send(pack, first.at[lo, core], sems, device(x, y, z, hi))

    copies.arrivals["first"] = (first, sems[1])
    gathers.append((sems[0], tiles, tiles.at[0 : NZ - 1]))

    loads[2].wait()
    waited.append(2)
    teach = teach_in[...].astype(F32)
    top_t = jnp.max(teach, axis=0, keepdims=True)
    total_t = jnp.sum(jnp.exp(teach - top_t), axis=0, keepdims=True)

    copies.arrive("first")

    sib_sems = [pair(sib_sem, t) for t in range(2)]
    for t in range(2):
        for j in range(NLO):
            left, right = first[j, 0].astype(F32), first[j, 1].astype(F32)
            rows = jnp.concatenate([left[8 * t : 8 * t + 8], right[8 * t : 8 * t + 8]], axis=0)
            lanes[t, :, 112 * j : 112 * (j + 1)] = rows[:, 0:112]
        block = hc.at[x, t, y, core]
        block[...] = lanes[t].astype(BF16)
        for x_, y_ in in_plane:
            send(block, block, (plane_send.at[t], plane_recv.at[t, me]), device(x_, y_, z, core))
        copies.departures[("plane", t)] = (hc.at[0:3, t, 0:4, 0], plane_send.at[t])
        send(block, block, sib_sems[t], sibling)
        copies.departures[("plane3", t)] = (hc.at[0:3, t, 0, 0], plane_send.at[t])
        for n, (x_, y_) in enumerate(in_plane):
            copies.arrivals[("plane", t, n)] = (hc.at[x_, t, y_, core], plane_recv.at[t, x_ * NY + y_])

    def to_sibling(t):
        for n, (x_, y_) in list(enumerate(in_plane))[::-1]:
            copies.arrive(("plane", t, n))
            block = hc.at[x_, t, y_, core]
            send(block, block, sib_sems[t], sibling)
        copies.expect(("sib", t), hc.at[0], sib_sems[t])

    copies.expect(("sib", 0), hc.at[0, 0, 0, 0], sib_sems[0])
    copies.expect(("sib", 1), hc.at[0, 0, 0, 0], sib_sems[1])
    to_sibling(0)
    copies.arrive(("sib", 0))

    loads[3].wait()
    waited.append(3)
    total = None
    for c in range(NX):
        states = hc[c, 0].reshape(128, 896)
        term = lax.dot_general(table[:, 896 * c : 896 * (c + 1)], states, CONTRACT_LAST, preferred_element_type=F32)
        total = term if total is None else total + term
    logits_ref[...] = total
    peak = jnp.max(total, axis=0, keepdims=True)
    weights = jnp.exp(total - peak)
    gap = total - teach
    stat_core[core] = tile_of(
        [peak, jnp.sum(weights, axis=0, keepdims=True), jnp.sum(weights * gap, axis=0, keepdims=True), top_t, total_t]
    )
    sems = pair(st_sem, 0)
    send(stat_core.at[core], stat_core.at[core], sems, sibling)
    copies.expect("st0", stat_core.at[0], sems)
    copies.arrive("st0")
    chip = merge_tiles(stat_core)
    stat_xy[me] = tile_of(chip)
    sems = pair(st_sem, 1)
    for x_, y_ in in_plane:
        send(stat_xy.at[me], stat_xy.at[me], sems, device(x_, y_, z, core))
    copies.expect("st1", stat_xy.at[0 : NXY - 1], sems)

    p = jnp.exp(total - chip[0])
    both = jnp.concatenate([(p * (gap - chip[2] / chip[1])).astype(BF16), p.astype(BF16)], axis=1)
    order = [lax.rem(x + i, NX) for i in (2, 1, 3, 0)]
    for i, c in enumerate(order):
        columns = table[:, pl.ds(pl.multiple_of(896 * c, 128), 896)]
        sums = lax.dot_general(both, columns, CONTRACT_FIRST, preferred_element_type=F32)
        part[i] = sums.astype(BF16).reshape(2, NY, NHI, 16, 896)
        sems = pair(rs0_sem, i)
        send(part.at[i, :, :, other], sib_part.at[i], sems, sibling)
        copies.expect(("rs0", i), sib_part.at[i], sems)
    sems = pair(rs1_sem)
    for i, c in enumerate(order):
        copies.arrive(("rs0", i))
        for r in range(NY):
            for k in range(2):
                t_ref[i, r, k] = (part[i, k, r, core].astype(F32) + sib_part[i, k, r].astype(F32)).astype(BF16)
        for j in (2, 1, 3, 0):
            y_ = lax.rem(y + j, NY)
            if i < 3 or j > 0:
                send(t_ref.at[i, y_], u_ref.at[me], sems, device(c, y_, z, core))
            else:
                u_ref[me] = t_ref[i, y_]
    copies.expect("rs1", u_ref.at[0 : NXY - 1], sems)

    copies.arrive("st1")
    stat_z[z] = tile_of(merge_tiles(stat_xy))
    sems = pair(st_sem, 2)
    for z_ in along_z:
        send(stat_z.at[z], stat_z.at[z], sems, device(x, y, z_, core))
    copies.expect("st2", stat_z.at[0 : NZ - 1], sems)
    to_sibling(1)
    copies.arrive("st2")
    peak_s, sum_s, cross, peak_t, sum_t = merge_tiles(stat_z)

    loads[4].wait()
    loads[5].wait()
    waited.extend([4, 5])
    log_zs = peak_s + jnp.log(sum_s)
    log_zt = peak_t + jnp.log(sum_t)
    kl_term = cross / sum_s - log_zs + log_zt
    weight = mask_in[...].astype(F32) / 128.0
    loss_ref[...] = jnp.broadcast_to(jnp.sum(weight * kl_term, axis=1, keepdims=True), loss_ref.shape)
    scale = weight / sum_s * jnp.exp(stat_xy[:, 0, :] - peak_s)
    shift = scale * (stat_xy[:, 2, :] / stat_xy[:, 1, :] - cross / sum_s)
    cols_ref[...] = jnp.concatenate([scale, shift, jnp.zeros((128 - 2 * NXY, 128), F32)], axis=0).T
    cols = cols_ref[pl.ds(pl.multiple_of(y * 32 + core * 16, 16), 16), :]

    copies.arrive("rs1")
    acc = jnp.zeros((16, 896), F32)
    for j in range(NXY):
        acc = acc + cols[:, j : j + 1] * u_ref[j, 0].astype(F32)
        acc = acc + cols[:, NXY + j : NXY + j + 1] * u_ref[j, 1].astype(F32)
    lanes[0] = acc
    z_src[...] = jnp.zeros_like(z_src)
    for j in range(NLO):
        for k in range(NCORE):
            z_src[j, k, :, 0:112] = lanes[0, 8 * k : 8 * k + 8, 112 * j : 112 * (j + 1)]

    sems = pair(rs2_sem)
    for j in (0, 7, 1, 6, 2, 5, 3, 4):
        lo_ = lax.rem(lo + j, NLO)
        send(z_src.at[lo_, other], z_dst.at[z], sems, device(x, y, core * NLO + lo_, other))
        if j > 0:
            send(z_src.at[lo_, core], z_dst.at[z], sems, device(x, y, core * NLO + lo_, core))
        else:

            @pl.when(core == hi)
            def _():
                pltpu.make_async_copy(z_src.at[lo, core], z_dst.at[z], sems[1]).start()

            @pl.when(core != hi)
            def _():
                send(z_src.at[lo, core], z_dst.at[z], sems, device(x, y, core * NLO + lo, core))

    copies.arrivals["rs2"] = (z_dst, sems[1])
    gathers.append((sems[0], z_dst, z_dst.at[0 : NZ - 1]))

    copies.arrive(("sib", 1))
    logits = logits_ref[...]
    prob = jnp.exp(logits - log_zs)
    inner = prob * (logits - teach_in[...].astype(F32) - log_zs + log_zt - kl_term)
    glog = (weight * inner).astype(BF16)
    rows = glog.shape[0]
    entries = (section * (NY * NHI * NCORE) + fsdp) * rows + lax.broadcasted_iota(jnp.int32, (rows, 128), 0)
    selector = (entries == ids_in[...]).astype(BF16)
    both = jnp.concatenate([glog, selector], axis=1)
    for c in range(NX):
        grad_ref[:, 896 * c : 896 * (c + 1)] = jnp.dot(
            both, hc[c].reshape(256, 896), preferred_element_type=F32
        ).astype(BF16)
    store = pltpu.make_async_copy(grad_ref, grad_hbm, store_sem)
    store.start()
    stores.append(store)
    copies.arrive("rs2")
    state_ref[...] = jnp.sum(z_dst[...], axis=0)[:, 0:112].astype(BF16)
    finish()


def shards(table, hidden_states, embed_cotangent, teacher_logits, student_ids, loss_mask):
    rows, width = table.shape
    tokens = teacher_logits.shape[1]
    block = hidden_states.shape
    vmem = pl.BlockSpec(memory_space=pltpu.VMEM)
    hbm = pl.BlockSpec(memory_space=pltpu.HBM)
    dma = pltpu.SemaphoreType.DMA
    table_grad, state_grad, loss = pl.pallas_call(
        kernel,
        out_shape=(
            jax.ShapeDtypeStruct((rows, width), BF16),
            jax.ShapeDtypeStruct(block, BF16),
            jax.ShapeDtypeStruct((1, 128), F32),
        ),
        in_specs=[hbm] * 6,
        out_specs=(pl.BlockSpec(memory_space=pl.ANY), vmem, vmem),
        scratch_shapes=[
            pltpu.VMEM((rows, width), BF16),
            pltpu.VMEM(block, BF16),
            pltpu.VMEM(block, BF16),
            pltpu.VMEM((rows, tokens), BF16),
            pltpu.VMEM((1, 128), jnp.int32),
            pltpu.VMEM((1, 128), jnp.int32),
            pltpu.VMEM((16, 128), BF16),
            pltpu.VMEM((NLO, NCORE, 16, 128), BF16),
            pltpu.VMEM((2, 16, 896), F32),
            pltpu.VMEM((NX, 2, NY, NHI, 16, 896), BF16),
            pltpu.VMEM((NCORE, 8, 128), F32),
            pltpu.VMEM((NXY, 8, 128), F32),
            pltpu.VMEM((NZ, 8, 128), F32),
            pltpu.VMEM((rows, tokens), F32),
            pltpu.VMEM((NX, 2, NY, NHI, 16, 896), BF16),
            pltpu.VMEM((NX, 2, NY, 16, 896), BF16),
            pltpu.VMEM((NX, NY, 2, 16, 896), BF16),
            pltpu.VMEM((NXY, 2, 16, 896), BF16),
            pltpu.VMEM((128, 128), F32),
            pltpu.VMEM((NLO, NCORE, 8, 128), F32),
            pltpu.VMEM((NZ, 8, 128), F32),
            pltpu.VMEM((rows, width), BF16),
            dma((6,)),
            dma,
            dma((2,)),
            dma((2,)),
            dma((2, NXY)),
            dma((2, 2)),
            dma((2, 3)),
            dma((2, NX)),
            dma((2,)),
            dma((2,)),
        ],
        compiler_params=pltpu.CompilerParams(
            collective_id=0, has_side_effects=True, vmem_limit_bytes=VMEM_MIB * 1024 * 1024
        ),
    )(
        table,
        hidden_states,
        embed_cotangent,
        teacher_logits,
        student_ids.reshape(1, 128),
        loss_mask.reshape(1, 128),
    )
    return table_grad, state_grad, loss[0, 0]


def solution(mesh):
    return jax.shard_map(
        shards,
        mesh=mesh,
        in_specs=(
            P(("section", "fsdp"), None),
            P("fsdp", "section"),
            P("fsdp", "section"),
            P(("section", "fsdp"), None),
            P(),
            P(),
        ),
        out_specs=(P(("section", "fsdp"), None), P("fsdp", "section"), P()),
        check_vma=False,
    )
```

```python
import functools

import jax
import jax.numpy as jnp
from jax import lax
from jax.experimental import pallas as pl
from jax.experimental.pallas import tpu as pltpu
from jax.sharding import PartitionSpec as P

MESH = pl.DeviceIdType.MESH
F32, BF16 = jnp.float32, jnp.bfloat16
CONTRACT_LAST = (((1,), (1,)), ((), ()))
CONTRACT_FIRST = (((0,), (0,)), ((), ()))
NX, NY, NLO, NHI, NCORE = 4, 4, 8, 2, 2
NZ = NLO * NHI
NXY = NX * NY
VMEM_MIB = 60
FAR_Z = sorted(range(1, NZ), key=lambda j: -min(j, NZ - j))
FAR_XY = sorted(
    ((i, j) for i in range(NX) for j in range(NY) if i or j), key=lambda d: -sum(min(v, 4 - v) for v in d)
)


def merge(maxes, *sums):
    top = jnp.max(maxes, axis=0, keepdims=True)
    scale = jnp.exp(maxes - top)
    return (top, *(jnp.sum(s * scale, axis=0, keepdims=True) for s in sums))


def merge_tiles(ref):
    peak_s, sum_s, cross = merge(ref[:, 0, :], ref[:, 1, :], ref[:, 2, :])
    peak_t, sum_t = merge(ref[:, 3, :], ref[:, 4, :])
    return peak_s, sum_s, cross, peak_t, sum_t


def tile_of(rows):
    return jnp.concatenate([*rows, jnp.zeros((3, rows[0].shape[1]), F32)], axis=0)


class Copies:
    def __init__(self):
        self.arrivals, self.departures = {}, {}

    @staticmethod
    def wait(ref, sem):
        pltpu.make_async_copy(ref, ref, sem).wait()

    @staticmethod
    def send(src, dst, sems, target):
        pltpu.make_async_remote_copy(
            src_ref=src, dst_ref=dst, send_sem=sems[0], recv_sem=sems[1], device_id=target, device_id_type=MESH
        ).start()

    def expect(self, key, ref, sems):
        self.arrivals[key] = (ref, sems[1])
        self.departures[key] = (ref, sems[0])

    def arrive(self, key):
        self.wait(*self.arrivals.pop(key))

    def finish(self):
        for key in list(self.arrivals):
            self.arrive(key)
        for ref, sem in self.departures.values():
            self.wait(ref, sem)


def kernel(
    table_hbm, hidden_hbm, cot_hbm, teach_hbm, ids_hbm, mask_hbm,
    grad_hbm, state_ref, loss_ref,
    table, hidden_in, cot_in, teach_in, ids_in, mask_in,
    pack, first, lanes, hc, stat_xy, stat_z, teach_ref, logits_ref,
    t_ref, u_ref, cols_ref, z_src, z_dst, g_out, g_all, loss_x, grad_ref,
    load_sem, store_sem, ag1_sem, pre_sem, plane_send, plane_recv, sib_sem, st_sem, rs1_sem, rs2_sem, g_sem,
):
    section, fsdp = lax.axis_index("section"), lax.axis_index("fsdp")
    x, lo = section // NLO, lax.rem(section, NLO)
    y, hi, core = fsdp // (NHI * NCORE), lax.rem(fsdp // NCORE, NHI), lax.rem(fsdp, NCORE)
    z, me = hi * NLO + lo, x * NY + y
    other = 1 - core

    def device(x_, y_, z_, core_):
        return (x_ * NLO + lax.rem(z_, NLO), y_ * (NHI * NCORE) + (z_ // NLO) * NCORE + core_)

    sibling = device(x, y, z, other)
    along_z = [lax.rem(z + j, NZ) for j in FAR_Z]
    in_plane = [(lax.rem(x + i, NX), lax.rem(y + j, NY)) for i, j in FAR_XY]
    copies = Copies()
    send = copies.send

    def pair(ref, *at):
        return ref.at[(0, *at)], ref.at[(1, *at)]

    def own_half(v):
        halves = [
            jnp.concatenate([v[:, 32 * q + 16 * h : 32 * q + 16 * h + 16] for q in range(NY)] * 2, axis=1)
            for h in range(2)
        ]
        return jnp.where(core == 0, halves[0], halves[1])

    def left_lanes(shape):
        return lax.broadcasted_iota(jnp.int32, shape, 1) < 64

    loads = [
        pltpu.make_async_copy(src, dst, load_sem.at[i])
        for i, (src, dst) in enumerate(
            [
                (hidden_hbm, hidden_in), (cot_hbm, cot_in), (teach_hbm, teach_in.at[core]),
                (table_hbm, table.at[core]), (ids_hbm, ids_in), (mask_hbm, mask_in),
            ]
        )
    ]
    loads[0].start()
    loads[1].start()

    barrier = pltpu.get_barrier_semaphore()
    for z_ in along_z:
        pl.semaphore_signal(barrier, inc=1, device_id=device(x, y, z_, core), device_id_type=MESH)
        pl.semaphore_signal(barrier, inc=1, device_id=device(x, y, z_, other), device_id_type=MESH)
    for x_, y_ in in_plane:
        pl.semaphore_signal(barrier, inc=1, device_id=device(x_, y_, z, core), device_id_type=MESH)
    pl.semaphore_signal(barrier, inc=1, device_id=sibling, device_id_type=MESH)
    for load in loads[2:]:
        load.start()

    loads[0].wait()
    loads[1].wait()
    pack[...] = jnp.zeros_like(pack)
    pack[:, 0:112] = jnp.concatenate([hidden_in[...].astype(F32), cot_in[...].astype(F32)], axis=0).astype(BF16)
    pl.semaphore_wait(barrier, 1 + 2 * (NZ - 1) + NXY - 1)

    sems = pair(ag1_sem)
    for z_ in along_z:
        send(pack, first.at[lo, core], sems, device(x, y, z_, hi))

    @pl.when(core == hi)
    def _():
        pltpu.make_async_copy(pack, first.at[lo, core], sems[1]).start()

    @pl.when(core != hi)
    def _():
        send(pack, first.at[lo, core], sems, device(x, y, z, hi))

    for i, (src, dst) in enumerate(((teach_hbm, teach_in), (table_hbm, table))):
        sems = pair(pre_sem, i)
        send(src, dst.at[core], sems, sibling)
        copies.expect(("pre", i), dst.at[0], sems)
    for load in loads[2:]:
        load.wait()
    copies.arrive(("pre", 0))
    for s in range(2):
        teach_ref[s] = own_half(teach_in[s].astype(F32))
    top_t = jnp.max(jnp.maximum(teach_ref[0], teach_ref[1]), axis=0, keepdims=True)
    total_t = jnp.sum(jnp.exp(teach_ref[0] - top_t) + jnp.exp(teach_ref[1] - top_t), axis=0, keepdims=True)
    weight = own_half(mask_in[...].astype(F32) / 128.0)

    copies.wait(first, ag1_sem.at[1])

    def share(t):
        block = hc.at[x, t, core, y]
        for x_, y_ in in_plane:
            send(block, block, (plane_send.at[t], plane_recv.at[t, me]), device(x_, y_, z, core))

    def gathered(t):
        for x_, y_ in in_plane[::-1]:
            copies.wait(hc.at[x_, t, core, y_], plane_recv.at[t, x_ * NY + y_])

    def to_sibling(t):
        half = hc.at[:, t, core]
        send(half, half, pair(sib_sem, t), sibling)
        copies.expect(("sib", t), half, pair(sib_sem, t))

    for t in range(2):
        for j in range(NLO):
            left, right = first[j, 0].astype(F32), first[j, 1].astype(F32)
            rows = jnp.concatenate([left[8 * t : 8 * t + 8], right[8 * t : 8 * t + 8]], axis=0)
            lanes[t, :, 112 * j : 112 * (j + 1)] = rows[:, 0:112]
        hc[x, t, core, y] = lanes[t].astype(BF16)
        if t == 0:
            share(0)
    gathered(0)
    copies.arrive(("pre", 1))
    total = [None, None]
    for c in range(NX):
        states = hc[c, 0, core].reshape(64, 896)
        states = jnp.concatenate([states, states], axis=0)
        for s in range(2):
            term = lax.dot_general(
                table[s, :, 896 * c : 896 * (c + 1)], states, CONTRACT_LAST, preferred_element_type=F32
            )
            total[s] = term if c == 0 else total[s] + term
    peak = jnp.max(jnp.maximum(total[0], total[1]), axis=0, keepdims=True)
    p = [jnp.exp(t - peak) for t in total]
    gap = [t - teach_ref[s] for s, t in enumerate(total)]
    chip_sum = jnp.sum(p[0] + p[1], axis=0, keepdims=True)
    chip_cross = jnp.sum(p[0] * gap[0] + p[1] * gap[1], axis=0, keepdims=True)
    stat_xy[me] = tile_of([peak, chip_sum, chip_cross, top_t, total_t])
    sems = pair(st_sem, 0)
    for x_, y_ in in_plane:
        send(stat_xy.at[me], stat_xy.at[me], sems, device(x_, y_, z, core))
    copies.expect("st1", stat_xy.at[0 : NXY - 1], sems)
    logits_ref[0] = total[0]
    logits_ref[1] = total[1]

    mean = chip_cross / chip_sum
    both = [
        jnp.where(left_lanes(p[s].shape), p[s] * (gap[s] - mean), p[s]).astype(BF16) for s in range(2)
    ]
    sems = pair(rs1_sem)
    for i, c in enumerate([lax.rem(x + i, NX) for i in (2, 1, 3, 0)]):
        at = pl.ds(pl.multiple_of(896 * c, 128), 896)
        sums = lax.dot_general(both[0], table[0, :, at], CONTRACT_FIRST, preferred_element_type=F32)
        sums = sums + lax.dot_general(both[1], table[1, :, at], CONTRACT_FIRST, preferred_element_type=F32)
        sums = sums.astype(BF16).reshape(2, NY, 16, 896)
        for r in range(NY):
            for k in range(2):
                t_ref[i, r, k] = sums[k, r]
        for j in (2, 1, 3, 0):
            y_ = lax.rem(y + j, NY)
            if i < 3 or j > 0:
                send(t_ref.at[i, y_], u_ref.at[me], sems, device(c, y_, z, core))
            else:
                u_ref[me] = t_ref[i, y_]
    copies.expect("rs1", u_ref.at[0 : NXY - 1], sems)
    share(1)

    copies.arrive("st1")
    stat_z[z] = tile_of(merge_tiles(stat_xy))
    sems = pair(st_sem, 1)
    for z_ in along_z:
        send(stat_z.at[z], stat_z.at[z], sems, device(x, y, z_, core))
    copies.expect("st2", stat_z.at[0 : NZ - 1], sems)
    to_sibling(0)
    copies.arrive("st2")
    peak_s, sum_s, cross, peak_t, sum_t = merge_tiles(stat_z)

    log_zs = peak_s + jnp.log(sum_s)
    log_zt = peak_t + jnp.log(sum_t)
    kl_term = cross / sum_s - log_zs + log_zt
    part = jnp.sum(jnp.where(left_lanes(weight.shape), weight * kl_term, 0.0), axis=1, keepdims=True)
    scale = weight / sum_s * jnp.exp(stat_xy[:, 0, :] - peak_s)
    shift = scale * (stat_xy[:, 2, :] / stat_xy[:, 1, :] - cross / sum_s)
    cols_ref[...] = jnp.concatenate([scale, shift, jnp.zeros((128 - 2 * NXY, 128), F32)], axis=0).T
    cols = cols_ref[pl.ds(pl.multiple_of(y * 16, 16), 16), :]

    copies.arrive("rs1")
    acc = jnp.zeros((16, 896), F32)
    for j in range(NXY):
        acc = acc + cols[:, j : j + 1] * u_ref[j, 0].astype(F32)
        acc = acc + cols[:, NXY + j : NXY + j + 1] * u_ref[j, 1].astype(F32)
    lanes[0] = acc
    z_src[...] = jnp.zeros_like(z_src)
    for j in range(NLO):
        for k in range(NCORE):
            z_src[j, k, :, 0:112] = lanes[0, 8 * k : 8 * k + 8, 112 * j : 112 * (j + 1)]

    sems = pair(rs2_sem)
    for j in (0, 7, 1, 6, 2, 5, 3, 4):
        lo_ = lax.rem(lo + j, NLO)
        send(z_src.at[lo_, other], z_dst.at[z], sems, device(x, y, core * NLO + lo_, other))
        if j > 0:
            send(z_src.at[lo_, core], z_dst.at[z], sems, device(x, y, core * NLO + lo_, core))
        else:

            @pl.when(core == hi)
            def _():
                pltpu.make_async_copy(z_src.at[lo, core], z_dst.at[z], sems[1]).start()

            @pl.when(core != hi)
            def _():
                send(z_src.at[lo, core], z_dst.at[z], sems, device(x, y, core * NLO + lo, core))

    def logits_grad(s):
        logits = logits_ref[s]
        inner = jnp.exp(logits - log_zs) * (logits - teach_ref[s] - log_zs + log_zt - kl_term)
        return (weight * inner).astype(BF16)

    loss_x[core] = jnp.broadcast_to(part, (8, 128))
    g_out[...] = logits_grad(other)
    for i, (src, dst) in enumerate(((g_out, g_all.at[core]), (loss_x.at[core], loss_x.at[core]))):
        send(src, dst, pair(g_sem, i), sibling)
        copies.expect(("g", i), dst, pair(g_sem, i))
    own = logits_grad(core)
    gathered(1)
    to_sibling(1)
    ids = ids_in[...]
    ids = jnp.concatenate([ids[:, 32 * q + 16 * h : 32 * q + 16 * h + 16] for h in range(2) for q in range(NY)], axis=1)
    rows = own.shape[0]
    entries = (section * (NY * NHI * NCORE) + fsdp) * rows + lax.broadcasted_iota(jnp.int32, (rows, 128), 0)
    selector = (entries == ids).astype(BF16)
    for i in range(2):
        copies.arrive(("g", i))
    for t in range(2):
        copies.arrive(("sib", t))
    loss_ref[...] = loss_x[0, 0:1] + loss_x[1, 0:1]
    mine = left_lanes(own.shape) == (core == 0)
    glog = jnp.where(mine, own.astype(F32), g_all[other].astype(F32)).astype(BF16)
    both = jnp.concatenate([glog, selector], axis=1)
    for c in range(NX):
        grad_ref[:, 896 * c : 896 * (c + 1)] = jnp.dot(
            both, hc[c].reshape(256, 896), preferred_element_type=F32
        ).astype(BF16)
    store = pltpu.make_async_copy(grad_ref, grad_hbm, store_sem)
    store.start()
    copies.wait(z_dst, rs2_sem.at[1])
    state_ref[...] = jnp.sum(z_dst[...], axis=0)[:, 0:112].astype(BF16)

    tiles = first.reshape(NZ, 16, 128)

    @pl.when(core == hi)
    def _():
        copies.wait(tiles.at[0 : NZ - 1], ag1_sem.at[0])
        copies.wait(z_dst.at[0 : NZ - 1], rs2_sem.at[0])

    @pl.when(core != hi)
    def _():
        copies.wait(tiles, ag1_sem.at[0])
        copies.wait(z_dst, rs2_sem.at[0])

    for t in range(2):
        copies.wait(hc.at[0:3, t, 0, 0:4], plane_send.at[t])
        copies.wait(hc.at[0:3, t, 0, 0], plane_send.at[t])
    copies.finish()
    store.wait()


def shards(table, hidden_states, embed_cotangent, teacher_logits, student_ids, loss_mask):
    rows, width = table.shape
    tokens = teacher_logits.shape[1]
    block = hidden_states.shape
    vmem = pl.BlockSpec(memory_space=pltpu.VMEM)
    hbm = pl.BlockSpec(memory_space=pltpu.HBM)
    dma = pltpu.SemaphoreType.DMA
    table_grad, state_grad, loss = pl.pallas_call(
        kernel,
        out_shape=(
            jax.ShapeDtypeStruct((rows, width), BF16),
            jax.ShapeDtypeStruct(block, BF16),
            jax.ShapeDtypeStruct((1, 128), F32),
        ),
        in_specs=[hbm] * 6,
        out_specs=(pl.BlockSpec(memory_space=pl.ANY), vmem, vmem),
        scratch_shapes=[
            pltpu.VMEM((NCORE, rows, width), BF16),
            pltpu.VMEM(block, BF16),
            pltpu.VMEM(block, BF16),
            pltpu.VMEM((NCORE, rows, tokens), BF16),
            pltpu.VMEM((1, 128), jnp.int32),
            pltpu.VMEM((1, 128), jnp.int32),
            pltpu.VMEM((16, 128), BF16),
            pltpu.VMEM((NLO, NCORE, 16, 128), BF16),
            pltpu.VMEM((2, 16, 896), F32),
            pltpu.VMEM((NX, 2, NHI, NY, 16, 896), BF16),
            pltpu.VMEM((NXY, 8, 128), F32),
            pltpu.VMEM((NZ, 8, 128), F32),
            pltpu.VMEM((NCORE, rows, tokens), F32),
            pltpu.VMEM((NCORE, rows, tokens), F32),
            pltpu.VMEM((NX, NY, 2, 16, 896), BF16),
            pltpu.VMEM((NXY, 2, 16, 896), BF16),
            pltpu.VMEM((128, 128), F32),
            pltpu.VMEM((NLO, NCORE, 8, 128), F32),
            pltpu.VMEM((NZ, 8, 128), F32),
            pltpu.VMEM((rows, tokens), BF16),
            pltpu.VMEM((NCORE, rows, tokens), BF16),
            pltpu.VMEM((NCORE, 8, 128), F32),
            pltpu.VMEM((rows, width), BF16),
            dma((6,)),
            dma,
            dma((2,)),
            dma((2, 2)),
            dma((2,)),
            dma((2, NXY)),
            dma((2, 2)),
            dma((2, 2)),
            dma((2,)),
            dma((2,)),
            dma((2, 2)),
        ],
        compiler_params=pltpu.CompilerParams(
            collective_id=0, has_side_effects=True, vmem_limit_bytes=VMEM_MIB * 1024 * 1024
        ),
    )(
        table,
        hidden_states,
        embed_cotangent,
        teacher_logits,
        student_ids.reshape(1, 128),
        loss_mask.reshape(1, 128),
    )
    return table_grad, state_grad, loss[0, 0]


def solution(mesh):
    return jax.shard_map(
        shards,
        mesh=mesh,
        in_specs=(
            P(("section", "fsdp"), None),
            P("fsdp", "section"),
            P("fsdp", "section"),
            P(("section", "fsdp"), None),
            P(),
            P(),
        ),
        out_specs=(P(("section", "fsdp"), None), P("fsdp", "section"), P()),
        check_vma=False,
    )
```

```python
import functools

import jax
import jax.numpy as jnp
from jax import lax
from jax.experimental import pallas as pl
from jax.experimental.pallas import tpu as pltpu
from jax.sharding import PartitionSpec as P

MESH = pl.DeviceIdType.MESH
F32, BF16 = jnp.float32, jnp.bfloat16
CONTRACT_LAST = (((1,), (1,)), ((), ()))
CONTRACT_FIRST = (((0,), (0,)), ((), ()))
NX, NY, NLO, NHI, NCORE = 4, 4, 8, 2, 2
NZ = NLO * NHI
NXY = NX * NY
VMEM_MIB = 60
FAR_Z = sorted(range(1, NZ), key=lambda j: -min(j, NZ - j))
FAR_XY = sorted(
    ((i, j) for i in range(NX) for j in range(NY) if i or j), key=lambda d: -sum(min(v, 4 - v) for v in d)
)


def merge(maxes, *sums):
    top = jnp.max(maxes, axis=0, keepdims=True)
    scale = jnp.exp(maxes - top)
    return (top, *(jnp.sum(s * scale, axis=0, keepdims=True) for s in sums))


def merge_tiles(ref):
    peak_s, sum_s, cross = merge(ref[:, 0, :], ref[:, 1, :], ref[:, 2, :])
    peak_t, sum_t = merge(ref[:, 3, :], ref[:, 4, :])
    return peak_s, sum_s, cross, peak_t, sum_t


def tile_of(rows):
    return jnp.concatenate([*rows, jnp.zeros((3, rows[0].shape[1]), F32)], axis=0)


class Copies:
    def __init__(self):
        self.arrivals, self.departures = {}, {}

    @staticmethod
    def wait(ref, sem):
        pltpu.make_async_copy(ref, ref, sem).wait()

    @staticmethod
    def send(src, dst, sems, target):
        pltpu.make_async_remote_copy(
            src_ref=src, dst_ref=dst, send_sem=sems[0], recv_sem=sems[1], device_id=target, device_id_type=MESH
        ).start()

    def expect(self, key, ref, sems):
        self.arrivals[key] = (ref, sems[1])
        self.departures[key] = (ref, sems[0])

    def arrive(self, key):
        self.wait(*self.arrivals.pop(key))

    def finish(self):
        for key in list(self.arrivals):
            self.arrive(key)
        for ref, sem in self.departures.values():
            self.wait(ref, sem)


def kernel(
    table_hbm, hidden_hbm, cot_hbm, teach_hbm, ids_hbm, mask_hbm,
    grad_hbm, state_ref, loss_ref,
    table, hidden_in, cot_in, teach_in, ids_in, mask_in,
    pack, first, lanes, hc, stat_xy, stat_z, teach_ref, logits_ref,
    t_ref, u_ref, cols_ref, z_src, z_dst, g_out, g_all, loss_x, grad_ref,
    load_sem, store_sem, ag1_sem, pre_sem, plane_send, plane_recv, sib_sem, st_sem, rs1_sem, rs2_sem, g_sem,
):
    section, fsdp = lax.axis_index("section"), lax.axis_index("fsdp")
    x, lo = section // NLO, lax.rem(section, NLO)
    y, hi, core = fsdp // (NHI * NCORE), lax.rem(fsdp // NCORE, NHI), lax.rem(fsdp, NCORE)
    z, me = hi * NLO + lo, x * NY + y
    other = 1 - core

    def device(x_, y_, z_, core_):
        return (x_ * NLO + lax.rem(z_, NLO), y_ * (NHI * NCORE) + (z_ // NLO) * NCORE + core_)

    sibling = device(x, y, z, other)
    along_z = [lax.rem(z + j, NZ) for j in FAR_Z]
    in_plane = [(lax.rem(x + i, NX), lax.rem(y + j, NY)) for i, j in FAR_XY]
    copies = Copies()
    send = copies.send

    def pair(ref, *at):
        return ref.at[(0, *at)], ref.at[(1, *at)]

    def own_half(v):
        halves = [
            jnp.concatenate([v[:, 32 * q + 16 * h : 32 * q + 16 * h + 16] for q in range(NY)] * 2, axis=1)
            for h in range(2)
        ]
        return jnp.where(core == 0, halves[0], halves[1])

    def left_lanes(shape):
        return lax.broadcasted_iota(jnp.int32, shape, 1) < 64

    loads = [
        pltpu.make_async_copy(src, dst, load_sem.at[i])
        for i, (src, dst) in enumerate(
            [
                (hidden_hbm, hidden_in), (cot_hbm, cot_in), (teach_hbm, teach_in.at[core]),
                (table_hbm, table.at[core]), (ids_hbm, ids_in), (mask_hbm, mask_in),
            ]
        )
    ]
    loads[0].start()
    loads[1].start()

    barrier = pltpu.get_barrier_semaphore()
    for z_ in along_z:
        pl.semaphore_signal(barrier, inc=1, device_id=device(x, y, z_, core), device_id_type=MESH)
        pl.semaphore_signal(barrier, inc=1, device_id=device(x, y, z_, other), device_id_type=MESH)
    for x_, y_ in in_plane:
        pl.semaphore_signal(barrier, inc=1, device_id=device(x_, y_, z, core), device_id_type=MESH)
    pl.semaphore_signal(barrier, inc=1, device_id=sibling, device_id_type=MESH)
    for load in loads[2:]:
        load.start()

    loads[0].wait()
    loads[1].wait()
    pack[...] = jnp.zeros_like(pack)
    pack[:, 0:112] = jnp.concatenate([hidden_in[...].astype(F32), cot_in[...].astype(F32)], axis=0).astype(BF16)
    pl.semaphore_wait(barrier, 1 + 2 * (NZ - 1) + NXY - 1)

    sems = pair(ag1_sem)
    for z_ in along_z:
        send(pack, first.at[lo, core], sems, device(x, y, z_, hi))

    @pl.when(core == hi)
    def _():
        pltpu.make_async_copy(pack, first.at[lo, core], sems[1]).start()

    @pl.when(core != hi)
    def _():
        send(pack, first.at[lo, core], sems, device(x, y, z, hi))

    for i, (src, dst) in enumerate(((teach_hbm, teach_in), (table_hbm, table))):
        sems = pair(pre_sem, i)
        send(src, dst.at[core], sems, sibling)
        copies.expect(("pre", i), dst.at[0], sems)
    for load in loads[2:]:
        load.wait()
    copies.arrive(("pre", 0))
    for s in range(2):
        teach_ref[s] = own_half(teach_in[s].astype(F32))
    top_t = jnp.max(jnp.maximum(teach_ref[0], teach_ref[1]), axis=0, keepdims=True)
    total_t = jnp.sum(jnp.exp(teach_ref[0] - top_t) + jnp.exp(teach_ref[1] - top_t), axis=0, keepdims=True)
    weight = own_half(mask_in[...].astype(F32) / 128.0)

    copies.wait(first, ag1_sem.at[1])

    def share(t):
        block = hc.at[x, t, core, y]
        for x_, y_ in in_plane:
            send(block, block, (plane_send.at[t], plane_recv.at[t, me]), device(x_, y_, z, core))

    def gathered(t):
        for x_, y_ in in_plane[::-1]:
            copies.wait(hc.at[x_, t, core, y_], plane_recv.at[t, x_ * NY + y_])

    def to_sibling(t):
        half = hc.at[:, t, core]
        send(half, half, pair(sib_sem, t), sibling)
        copies.expect(("sib", t), half, pair(sib_sem, t))

    for t in range(2):
        for j in range(NLO):
            left, right = first[j, 0].astype(F32), first[j, 1].astype(F32)
            rows = jnp.concatenate([left[8 * t : 8 * t + 8], right[8 * t : 8 * t + 8]], axis=0)
            lanes[t, :, 112 * j : 112 * (j + 1)] = rows[:, 0:112]
        hc[x, t, core, y] = lanes[t].astype(BF16)
        if t == 0:
            share(0)
    copies.arrive(("pre", 1))
    total = [None, None]
    for i in (0, 1, 3, 2):
        c = lax.rem(x + i, NX)
        for j in (0, 1, 3, 2):
            if i or j:
                y_ = lax.rem(y + j, NY)
                copies.wait(hc.at[c, 0, core, y_], plane_recv.at[0, c * NY + y_])
        states = hc[c, 0, core].reshape(64, 896)
        states = jnp.concatenate([states, states], axis=0)
        at = pl.ds(pl.multiple_of(896 * c, 128), 896)
        for s in range(2):
            term = lax.dot_general(table[s, :, at], states, CONTRACT_LAST, preferred_element_type=F32)
            total[s] = term if i == 0 else total[s] + term
    peak = jnp.max(jnp.maximum(total[0], total[1]), axis=0, keepdims=True)
    p = [jnp.exp(t - peak) for t in total]
    gap = [t - teach_ref[s] for s, t in enumerate(total)]
    chip_sum = jnp.sum(p[0] + p[1], axis=0, keepdims=True)
    chip_cross = jnp.sum(p[0] * gap[0] + p[1] * gap[1], axis=0, keepdims=True)
    stat_xy[me] = tile_of([peak, chip_sum, chip_cross, top_t, total_t])
    sems = pair(st_sem, 0)
    for x_, y_ in in_plane:
        send(stat_xy.at[me], stat_xy.at[me], sems, device(x_, y_, z, core))
    copies.expect("st1", stat_xy.at[0 : NXY - 1], sems)
    logits_ref[0] = total[0]
    logits_ref[1] = total[1]

    mean = chip_cross / chip_sum
    both = [
        jnp.where(left_lanes(p[s].shape), p[s] * (gap[s] - mean), p[s]).astype(BF16) for s in range(2)
    ]
    sems = pair(rs1_sem)
    for i, c in enumerate([lax.rem(x + i, NX) for i in (2, 1, 3, 0)]):
        at = pl.ds(pl.multiple_of(896 * c, 128), 896)
        sums = lax.dot_general(both[0], table[0, :, at], CONTRACT_FIRST, preferred_element_type=F32)
        sums = sums + lax.dot_general(both[1], table[1, :, at], CONTRACT_FIRST, preferred_element_type=F32)
        sums = sums.astype(BF16).reshape(2, NY, 16, 896)
        for r in range(NY):
            for k in range(2):
                t_ref[i, r, k] = sums[k, r]
        for j in (2, 1, 3, 0):
            y_ = lax.rem(y + j, NY)
            if i < 3 or j > 0:
                send(t_ref.at[i, y_], u_ref.at[me], sems, device(c, y_, z, core))
            else:
                u_ref[me] = t_ref[i, y_]
    copies.expect("rs1", u_ref.at[0 : NXY - 1], sems)
    share(1)

    copies.arrive("st1")
    stat_z[z] = tile_of(merge_tiles(stat_xy))
    sems = pair(st_sem, 1)
    for z_ in along_z:
        send(stat_z.at[z], stat_z.at[z], sems, device(x, y, z_, core))
    copies.expect("st2", stat_z.at[0 : NZ - 1], sems)
    to_sibling(0)
    copies.arrive("st2")
    peak_s, sum_s, cross, peak_t, sum_t = merge_tiles(stat_z)

    log_zs = peak_s + jnp.log(sum_s)
    log_zt = peak_t + jnp.log(sum_t)
    kl_term = cross / sum_s - log_zs + log_zt
    part = jnp.sum(jnp.where(left_lanes(weight.shape), weight * kl_term, 0.0), axis=1, keepdims=True)
    scale = weight / sum_s * jnp.exp(stat_xy[:, 0, :] - peak_s)
    shift = scale * (stat_xy[:, 2, :] / stat_xy[:, 1, :] - cross / sum_s)
    cols_ref[...] = jnp.concatenate([scale, shift, jnp.zeros((128 - 2 * NXY, 128), F32)], axis=0).T
    cols = cols_ref[pl.ds(pl.multiple_of(y * 16, 16), 16), :]

    copies.arrive("rs1")
    acc = jnp.zeros((16, 896), F32)
    for j in range(NXY):
        acc = acc + cols[:, j : j + 1] * u_ref[j, 0].astype(F32)
        acc = acc + cols[:, NXY + j : NXY + j + 1] * u_ref[j, 1].astype(F32)
    lanes[0] = acc
    z_src[...] = jnp.zeros_like(z_src)
    for j in range(NLO):
        for k in range(NCORE):
            z_src[j, k, :, 0:112] = lanes[0, 8 * k : 8 * k + 8, 112 * j : 112 * (j + 1)]

    sems = pair(rs2_sem)
    for j in (0, 7, 1, 6, 2, 5, 3, 4):
        lo_ = lax.rem(lo + j, NLO)
        send(z_src.at[lo_, other], z_dst.at[z], sems, device(x, y, core * NLO + lo_, other))
        if j > 0:
            send(z_src.at[lo_, core], z_dst.at[z], sems, device(x, y, core * NLO + lo_, core))
        else:

            @pl.when(core == hi)
            def _():
                pltpu.make_async_copy(z_src.at[lo, core], z_dst.at[z], sems[1]).start()

            @pl.when(core != hi)
            def _():
                send(z_src.at[lo, core], z_dst.at[z], sems, device(x, y, core * NLO + lo, core))

    def logits_grad(s):
        logits = logits_ref[s]
        inner = jnp.exp(logits - log_zs) * (logits - teach_ref[s] - log_zs + log_zt - kl_term)
        return (weight * inner).astype(BF16)

    loss_x[core] = jnp.broadcast_to(part, (8, 128))
    g_out[...] = logits_grad(other)
    for i, (src, dst) in enumerate(((g_out, g_all.at[core]), (loss_x.at[core], loss_x.at[core]))):
        send(src, dst, pair(g_sem, i), sibling)
        copies.expect(("g", i), dst, pair(g_sem, i))
    own = logits_grad(core)
    gathered(1)
    to_sibling(1)
    ids = ids_in[...]
    ids = jnp.concatenate([ids[:, 32 * q + 16 * h : 32 * q + 16 * h + 16] for h in range(2) for q in range(NY)], axis=1)
    rows = own.shape[0]
    entries = (section * (NY * NHI * NCORE) + fsdp) * rows + lax.broadcasted_iota(jnp.int32, (rows, 128), 0)
    selector = (entries == ids).astype(BF16)
    for i in range(2):
        copies.arrive(("g", i))
    for t in range(2):
        copies.arrive(("sib", t))
    loss_ref[...] = loss_x[0, 0:1] + loss_x[1, 0:1]
    mine = left_lanes(own.shape) == (core == 0)
    glog = jnp.where(mine, own.astype(F32), g_all[other].astype(F32)).astype(BF16)
    both = jnp.concatenate([glog, selector], axis=1)
    for c in range(NX):
        grad_ref[:, 896 * c : 896 * (c + 1)] = jnp.dot(
            both, hc[c].reshape(256, 896), preferred_element_type=F32
        ).astype(BF16)
    store = pltpu.make_async_copy(grad_ref, grad_hbm, store_sem)
    store.start()
    copies.wait(z_dst, rs2_sem.at[1])
    state_ref[...] = jnp.sum(z_dst[...], axis=0)[:, 0:112].astype(BF16)

    tiles = first.reshape(NZ, 16, 128)

    @pl.when(core == hi)
    def _():
        copies.wait(tiles.at[0 : NZ - 1], ag1_sem.at[0])
        copies.wait(z_dst.at[0 : NZ - 1], rs2_sem.at[0])

    @pl.when(core != hi)
    def _():
        copies.wait(tiles, ag1_sem.at[0])
        copies.wait(z_dst, rs2_sem.at[0])

    for t in range(2):
        copies.wait(hc.at[0:3, t, 0, 0:4], plane_send.at[t])
        copies.wait(hc.at[0:3, t, 0, 0], plane_send.at[t])
    copies.finish()
    store.wait()


def hand_over(grad, state, loss, grad_out, state_out, loss_out, grad_v, state_v, loss_v, in_sem, out_sem):
    parts = [(grad.at[:, at], grad_v.at[:, at], grad_out.at[:, at]) for at in (pl.ds(896 * c, 896) for c in range(NX))]
    parts = [(state, state_v, state_out), (loss, loss_v, loss_out), *parts]
    loads = [pltpu.make_async_copy(src, via, in_sem.at[i]) for i, (src, via, _) in enumerate(parts)]
    stores = [pltpu.make_async_copy(via, dst, out_sem.at[i]) for i, (_, via, dst) in enumerate(parts)]
    for load in loads:
        load.start()
    for load, store in zip(loads, stores):
        load.wait()
        store.start()
    for store in stores:
        store.wait()


def shards(table, hidden_states, embed_cotangent, teacher_logits, student_ids, loss_mask):
    rows, width = table.shape
    tokens = teacher_logits.shape[1]
    block = hidden_states.shape
    vmem = pl.BlockSpec(memory_space=pltpu.VMEM)
    hbm = pl.BlockSpec(memory_space=pltpu.HBM)
    dma = pltpu.SemaphoreType.DMA
    table_grad, state_grad, loss = pl.pallas_call(
        kernel,
        out_shape=(
            jax.ShapeDtypeStruct((rows, width), BF16),
            jax.ShapeDtypeStruct(block, BF16),
            jax.ShapeDtypeStruct((1, 128), F32),
        ),
        in_specs=[hbm] * 6,
        out_specs=(pl.BlockSpec(memory_space=pl.ANY), vmem, vmem),
        scratch_shapes=[
            pltpu.VMEM((NCORE, rows, width), BF16),
            pltpu.VMEM(block, BF16),
            pltpu.VMEM(block, BF16),
            pltpu.VMEM((NCORE, rows, tokens), BF16),
            pltpu.VMEM((1, 128), jnp.int32),
            pltpu.VMEM((1, 128), jnp.int32),
            pltpu.VMEM((16, 128), BF16),
            pltpu.VMEM((NLO, NCORE, 16, 128), BF16),
            pltpu.VMEM((2, 16, 896), F32),
            pltpu.VMEM((NX, 2, NHI, NY, 16, 896), BF16),
            pltpu.VMEM((NXY, 8, 128), F32),
            pltpu.VMEM((NZ, 8, 128), F32),
            pltpu.VMEM((NCORE, rows, tokens), F32),
            pltpu.VMEM((NCORE, rows, tokens), F32),
            pltpu.VMEM((NX, NY, 2, 16, 896), BF16),
            pltpu.VMEM((NXY, 2, 16, 896), BF16),
            pltpu.VMEM((128, 128), F32),
            pltpu.VMEM((NLO, NCORE, 8, 128), F32),
            pltpu.VMEM((NZ, 8, 128), F32),
            pltpu.VMEM((rows, tokens), BF16),
            pltpu.VMEM((NCORE, rows, tokens), BF16),
            pltpu.VMEM((NCORE, 8, 128), F32),
            pltpu.VMEM((rows, width), BF16),
            dma((6,)),
            dma,
            dma((2,)),
            dma((2, 2)),
            dma((2,)),
            dma((2, NXY)),
            dma((2, 2)),
            dma((2, 2)),
            dma((2,)),
            dma((2,)),
            dma((2, 2)),
        ],
        compiler_params=pltpu.CompilerParams(
            collective_id=0, has_side_effects=True, vmem_limit_bytes=VMEM_MIB * 1024 * 1024
        ),
    )(
        table,
        hidden_states,
        embed_cotangent,
        teacher_logits,
        student_ids.reshape(1, 128),
        loss_mask.reshape(1, 128),
    )
    results = (table_grad, state_grad, loss)
    table_grad, state_grad, loss = pl.pallas_call(
        hand_over,
        out_shape=[jax.ShapeDtypeStruct(r.shape, r.dtype) for r in results],
        in_specs=[pl.BlockSpec(memory_space=pl.ANY)] * 3,
        out_specs=[pl.BlockSpec(memory_space=pl.ANY)] * 3,
        scratch_shapes=[*(pltpu.VMEM(r.shape, r.dtype) for r in results), dma((NX + 2,)), dma((NX + 2,))],
        compiler_params=pltpu.CompilerParams(vmem_limit_bytes=VMEM_MIB * 1024 * 1024),
    )(*results)
    return table_grad, state_grad, loss[0, 0]


def solution(mesh):
    return jax.shard_map(
        shards,
        mesh=mesh,
        in_specs=(
            P(("section", "fsdp"), None),
            P("fsdp", "section"),
            P("fsdp", "section"),
            P(("section", "fsdp"), None),
            P(),
            P(),
        ),
        out_specs=(P(("section", "fsdp"), None), P("fsdp", "section"), P()),
        check_vma=False,
    )
```

```python
import functools

import jax
import jax.numpy as jnp
from jax import lax
from jax.experimental import pallas as pl
from jax.experimental.pallas import tpu as pltpu
from jax.sharding import PartitionSpec as P

MESH = pl.DeviceIdType.MESH
F32, BF16 = jnp.float32, jnp.bfloat16
CONTRACT_LAST = (((1,), (1,)), ((), ()))
CONTRACT_FIRST = (((0,), (0,)), ((), ()))
NX, NY, NLO, NHI, NCORE = 4, 4, 8, 2, 2
NZ = NLO * NHI
NXY = NX * NY
VMEM_MIB = 60
FAR_Z = sorted(range(1, NZ), key=lambda j: -min(j, NZ - j))
FAR_XY = sorted(
    ((i, j) for i in range(NX) for j in range(NY) if i or j), key=lambda d: -sum(min(v, 4 - v) for v in d)
)


def merge(maxes, *sums):
    top = jnp.max(maxes, axis=0, keepdims=True)
    scale = jnp.exp(maxes - top)
    return (top, *(jnp.sum(s * scale, axis=0, keepdims=True) for s in sums))


def merge_tiles(ref):
    return merge(ref[:, 0, :], ref[:, 1, :], ref[:, 2, :])


def tile_of(rows):
    return jnp.concatenate([*rows, jnp.zeros((1, 128), F32)], axis=0)


class Copies:
    def __init__(self):
        self.arrivals, self.departures = {}, {}

    @staticmethod
    def wait(ref, sem):
        pltpu.make_async_copy(ref, ref, sem).wait()

    @staticmethod
    def send(src, dst, sems, target):
        pltpu.make_async_remote_copy(
            src_ref=src, dst_ref=dst, send_sem=sems[0], recv_sem=sems[1], device_id=target, device_id_type=MESH
        ).start()

    def expect(self, key, ref, sems):
        self.arrivals[key] = (ref, sems[1])
        self.departures[key] = (ref, sems[0])

    def arrive(self, key):
        self.wait(*self.arrivals.pop(key))

    def finish(self):
        for key in list(self.arrivals):
            self.arrive(key)
        for ref, sem in self.departures.values():
            self.wait(ref, sem)


def kernel(
    table_hbm, hidden_hbm, cot_hbm, teach_hbm, ids_hbm, mask_hbm,
    grad_hbm, state_ref, loss_ref,
    table, hidden_in, cot_in, teach_in, ids_in, mask_in,
    pack, first, lanes, hc, stat_xy, stat_z, teach_ref, logits_ref,
    t_ref, u_ref, cols_ref, z_src, z_dst, g_out, g_all, loss_x, grad_ref,
    load_sem, store_sem, ag1_sem, pre_sem, plane_send, plane_recv, sib_sem, st_sem, rs1_sem, rs2_sem, g_sem,
):
    section, fsdp = lax.axis_index("section"), lax.axis_index("fsdp")
    x, lo = section // NLO, lax.rem(section, NLO)
    y, hi, core = fsdp // (NHI * NCORE), lax.rem(fsdp // NCORE, NHI), lax.rem(fsdp, NCORE)
    z, me = hi * NLO + lo, x * NY + y
    other = 1 - core

    def device(x_, y_, z_, core_):
        return (x_ * NLO + lax.rem(z_, NLO), y_ * (NHI * NCORE) + (z_ // NLO) * NCORE + core_)

    sibling = device(x, y, z, other)
    along_z = [lax.rem(z + j, NZ) for j in FAR_Z]
    in_plane = [(lax.rem(x + i, NX), lax.rem(y + j, NY)) for i, j in FAR_XY]
    copies = Copies()
    send = copies.send

    def pair(ref, *at):
        return ref.at[(0, *at)], ref.at[(1, *at)]

    def own_half(v):
        halves = [
            jnp.concatenate([v[:, 32 * q + 16 * h : 32 * q + 16 * h + 16] for q in range(NY)] * 2, axis=1)
            for h in range(2)
        ]
        return jnp.where(core == 0, halves[0], halves[1])

    def left_lanes(shape):
        return lax.broadcasted_iota(jnp.int32, shape, 1) < 64

    loads = [
        pltpu.make_async_copy(src, dst, load_sem.at[i])
        for i, (src, dst) in enumerate(
            [
                (hidden_hbm, hidden_in), (cot_hbm, cot_in), (teach_hbm, teach_in.at[core]),
                (table_hbm, table.at[core]), (ids_hbm, ids_in), (mask_hbm, mask_in),
            ]
        )
    ]
    loads[0].start()
    loads[1].start()

    barrier = pltpu.get_barrier_semaphore()
    for z_ in along_z:
        pl.semaphore_signal(barrier, inc=1, device_id=device(x, y, z_, core), device_id_type=MESH)
        pl.semaphore_signal(barrier, inc=1, device_id=device(x, y, z_, other), device_id_type=MESH)
    for x_, y_ in in_plane:
        pl.semaphore_signal(barrier, inc=1, device_id=device(x_, y_, z, core), device_id_type=MESH)
    pl.semaphore_signal(barrier, inc=1, device_id=sibling, device_id_type=MESH)
    for load in loads[2:]:
        load.start()

    loads[0].wait()
    loads[1].wait()
    pack[...] = jnp.zeros_like(pack)
    pack[:, 0:112] = jnp.concatenate([hidden_in[...].astype(F32), cot_in[...].astype(F32)], axis=0).astype(BF16)
    pl.semaphore_wait(barrier, 1 + 2 * (NZ - 1) + NXY - 1)

    sems = pair(ag1_sem)
    for z_ in along_z:
        send(pack, first.at[lo, core], sems, device(x, y, z_, hi))

    @pl.when(core == hi)
    def _():
        pltpu.make_async_copy(pack, first.at[lo, core], sems[1]).start()

    @pl.when(core != hi)
    def _():
        send(pack, first.at[lo, core], sems, device(x, y, z, hi))

    for i, (src, dst) in enumerate(((teach_hbm, teach_in), (table_hbm, table))):
        sems = pair(pre_sem, i)
        send(src, dst.at[core], sems, sibling)
        copies.expect(("pre", i), dst.at[0], sems)
    for load in loads[2:]:
        load.wait()
    copies.arrive(("pre", 0))
    for s in range(2):
        teach_ref[s] = own_half(teach_in[s].astype(F32))
    top_t = jnp.max(jnp.maximum(teach_ref[0], teach_ref[1]), axis=0, keepdims=True)
    total_t = jnp.sum(jnp.exp(teach_ref[0] - top_t) + jnp.exp(teach_ref[1] - top_t), axis=0, keepdims=True)
    weight = own_half(mask_in[...].astype(F32) / 128.0)

    copies.wait(first, ag1_sem.at[1])

    def share(t):
        block = hc.at[x, t, core, y]
        for x_, y_ in in_plane:
            send(block, block, (plane_send.at[t], plane_recv.at[t, me]), device(x_, y_, z, core))

    def gathered(t):
        for x_, y_ in in_plane[::-1]:
            copies.wait(hc.at[x_, t, core, y_], plane_recv.at[t, x_ * NY + y_])

    def to_sibling(t):
        half = hc.at[:, t, core]
        send(half, half, pair(sib_sem, t), sibling)
        copies.expect(("sib", t), half, pair(sib_sem, t))

    for t in range(2):
        for j in range(NLO):
            left, right = first[j, 0].astype(F32), first[j, 1].astype(F32)
            rows = jnp.concatenate([left[8 * t : 8 * t + 8], right[8 * t : 8 * t + 8]], axis=0)
            lanes[t, :, 112 * j : 112 * (j + 1)] = rows[:, 0:112]
        hc[x, t, core, y] = lanes[t].astype(BF16)
        if t == 0:
            share(0)
    copies.arrive(("pre", 1))
    total = [None, None]
    for i in (0, 1, 3, 2):
        c = lax.rem(x + i, NX)
        for j in (0, 1, 3, 2):
            if i or j:
                y_ = lax.rem(y + j, NY)
                copies.wait(hc.at[c, 0, core, y_], plane_recv.at[0, c * NY + y_])
        states = hc[c, 0, core].reshape(64, 896)
        states = jnp.concatenate([states, states], axis=0)
        at = pl.ds(pl.multiple_of(896 * c, 128), 896)
        for s in range(2):
            term = lax.dot_general(table[s, :, at], states, CONTRACT_LAST, preferred_element_type=F32)
            total[s] = term if i == 0 else total[s] + term
    peak = jnp.max(jnp.maximum(total[0], total[1]), axis=0, keepdims=True)
    p = [jnp.exp(t - peak) for t in total]
    gap = [t - teach_ref[s] for s, t in enumerate(total)]
    chip_sum = jnp.sum(p[0] + p[1], axis=0, keepdims=True)
    chip_cross = jnp.sum(p[0] * gap[0] + p[1] * gap[1], axis=0, keepdims=True)
    left = left_lanes(peak.shape)
    stat_xy[me] = tile_of([jnp.where(left, peak, top_t), jnp.where(left, chip_sum, total_t), jnp.where(left, chip_cross, 0.0)])
    sems = pair(st_sem, 0)
    for x_, y_ in in_plane:
        send(stat_xy.at[me], stat_xy.at[me], sems, device(x_, y_, z, core))
    copies.expect("st1", stat_xy.at[0 : NXY - 1], sems)
    logits_ref[0] = total[0]
    logits_ref[1] = total[1]

    mean = chip_cross / chip_sum
    both = [
        jnp.where(left_lanes(p[s].shape), p[s] * (gap[s] - mean), p[s]).astype(BF16) for s in range(2)
    ]
    sems = pair(rs1_sem)
    for i, c in enumerate([lax.rem(x + i, NX) for i in (2, 1, 3, 0)]):
        at = pl.ds(pl.multiple_of(896 * c, 128), 896)
        sums = lax.dot_general(both[0], table[0, :, at], CONTRACT_FIRST, preferred_element_type=F32)
        sums = sums + lax.dot_general(both[1], table[1, :, at], CONTRACT_FIRST, preferred_element_type=F32)
        sums = sums.astype(BF16).reshape(2, NY, 16, 896)
        for r in range(NY):
            for k in range(2):
                t_ref[i, r, k] = sums[k, r]
        for j in (2, 1, 3, 0):
            y_ = lax.rem(y + j, NY)
            if i < 3 or j > 0:
                send(t_ref.at[i, y_], u_ref.at[me], sems, device(c, y_, z, core))
            else:
                u_ref[me] = t_ref[i, y_]
    copies.expect("rs1", u_ref.at[0 : NXY - 1], sems)

    copies.arrive("st1")
    stat_z[z] = tile_of(merge_tiles(stat_xy))
    sems = pair(st_sem, 1)
    for z_ in along_z:
        send(stat_z.at[z], stat_z.at[z], sems, device(x, y, z_, core))
    copies.expect("st2", stat_z.at[0 : NZ - 1], sems)
    share(1)
    to_sibling(0)
    copies.arrive("st2")
    merged = merge_tiles(stat_z)
    swapped = [jnp.concatenate([v[:, 64:128], v[:, 0:64]], axis=1) for v in merged]
    peak_s, sum_s, cross = (jnp.where(left, v, w) for v, w in zip(merged, swapped, strict=True))
    peak_t, sum_t = (jnp.where(left, w, v) for v, w in zip(merged[:2], swapped[:2], strict=True))

    log_zs = peak_s + jnp.log(sum_s)
    log_zt = peak_t + jnp.log(sum_t)
    kl_term = cross / sum_s - log_zs + log_zt
    part = jnp.sum(jnp.where(left_lanes(weight.shape), weight * kl_term, 0.0), axis=1, keepdims=True)
    scale = weight / sum_s * jnp.exp(stat_xy[:, 0, :] - peak_s)
    shift = scale * (stat_xy[:, 2, :] / stat_xy[:, 1, :] - cross / sum_s)
    cols_ref[...] = jnp.concatenate([scale, shift, jnp.zeros((128 - 2 * NXY, 128), F32)], axis=0).T
    cols = cols_ref[pl.ds(pl.multiple_of(y * 16, 16), 16), :]

    copies.arrive("rs1")
    acc = jnp.zeros((16, 896), F32)
    for j in range(NXY):
        acc = acc + cols[:, j : j + 1] * u_ref[j, 0].astype(F32)
        acc = acc + cols[:, NXY + j : NXY + j + 1] * u_ref[j, 1].astype(F32)
    lanes[0] = acc
    z_src[...] = jnp.zeros_like(z_src)
    for j in range(NLO):
        for k in range(NCORE):
            z_src[j, k, :, 0:112] = lanes[0, 8 * k : 8 * k + 8, 112 * j : 112 * (j + 1)]

    sems = pair(rs2_sem)
    for j in (0, 7, 1, 6, 2, 5, 3, 4):
        lo_ = lax.rem(lo + j, NLO)
        send(z_src.at[lo_, other], z_dst.at[z], sems, device(x, y, core * NLO + lo_, other))
        if j > 0:
            send(z_src.at[lo_, core], z_dst.at[z], sems, device(x, y, core * NLO + lo_, core))
        else:

            @pl.when(core == hi)
            def _():
                pltpu.make_async_copy(z_src.at[lo, core], z_dst.at[z], sems[1]).start()

            @pl.when(core != hi)
            def _():
                send(z_src.at[lo, core], z_dst.at[z], sems, device(x, y, core * NLO + lo, core))

    def logits_grad(s):
        logits = logits_ref[s]
        inner = jnp.exp(logits - log_zs) * (logits - teach_ref[s] - log_zs + log_zt - kl_term)
        return (weight * inner).astype(BF16)

    loss_x[core] = jnp.broadcast_to(part, (8, 128))
    g_out[...] = logits_grad(other)
    for i, (src, dst) in enumerate(((g_out, g_all.at[core]), (loss_x.at[core], loss_x.at[core]))):
        send(src, dst, pair(g_sem, i), sibling)
        copies.expect(("g", i), dst, pair(g_sem, i))
    own = logits_grad(core)
    gathered(1)
    to_sibling(1)
    ids = ids_in[...]
    ids = jnp.concatenate([ids[:, 32 * q + 16 * h : 32 * q + 16 * h + 16] for h in range(2) for q in range(NY)], axis=1)
    rows = own.shape[0]
    entries = (section * (NY * NHI * NCORE) + fsdp) * rows + lax.broadcasted_iota(jnp.int32, (rows, 128), 0)
    selector = (entries == ids).astype(BF16)
    for i in range(2):
        copies.arrive(("g", i))
    for t in range(2):
        copies.arrive(("sib", t))
    loss_ref[...] = loss_x[0, 0:1] + loss_x[1, 0:1]
    mine = left_lanes(own.shape) == (core == 0)
    glog = jnp.where(mine, own.astype(F32), g_all[other].astype(F32)).astype(BF16)
    both = jnp.concatenate([glog, selector], axis=1)
    for c in range(NX):
        grad_ref[:, 896 * c : 896 * (c + 1)] = jnp.dot(
            both, hc[c].reshape(256, 896), preferred_element_type=F32
        ).astype(BF16)
    store = pltpu.make_async_copy(grad_ref, grad_hbm, store_sem)
    store.start()
    copies.wait(z_dst, rs2_sem.at[1])
    state_ref[...] = jnp.sum(z_dst[...], axis=0)[:, 0:112].astype(BF16)

    tiles = first.reshape(NZ, 16, 128)

    @pl.when(core == hi)
    def _():
        copies.wait(tiles.at[0 : NZ - 1], ag1_sem.at[0])
        copies.wait(z_dst.at[0 : NZ - 1], rs2_sem.at[0])

    @pl.when(core != hi)
    def _():
        copies.wait(tiles, ag1_sem.at[0])
        copies.wait(z_dst, rs2_sem.at[0])

    for t in range(2):
        copies.wait(hc.at[0:3, t, 0, 0:4], plane_send.at[t])
        copies.wait(hc.at[0:3, t, 0, 0], plane_send.at[t])
    copies.finish()
    store.wait()


def hand_over(grad, state, loss, grad_out, state_out, loss_out, grad_v, state_v, loss_v, in_sem, out_sem):
    parts = [(grad.at[:, at], grad_v.at[:, at], grad_out.at[:, at]) for at in (pl.ds(896 * c, 896) for c in range(NX))]
    parts = [(state, state_v, state_out), (loss, loss_v, loss_out), *parts]
    loads = [pltpu.make_async_copy(src, via, in_sem.at[i]) for i, (src, via, _) in enumerate(parts)]
    stores = [pltpu.make_async_copy(via, dst, out_sem.at[i]) for i, (_, via, dst) in enumerate(parts)]
    for load in loads:
        load.start()
    for load, store in zip(loads, stores):
        load.wait()
        store.start()
    for store in stores:
        store.wait()


def shards(table, hidden_states, embed_cotangent, teacher_logits, student_ids, loss_mask):
    rows, width = table.shape
    tokens = teacher_logits.shape[1]
    block = hidden_states.shape
    vmem = pl.BlockSpec(memory_space=pltpu.VMEM)
    hbm = pl.BlockSpec(memory_space=pltpu.HBM)
    dma = pltpu.SemaphoreType.DMA
    table_grad, state_grad, loss = pl.pallas_call(
        kernel,
        out_shape=(
            jax.ShapeDtypeStruct((rows, width), BF16),
            jax.ShapeDtypeStruct(block, BF16),
            jax.ShapeDtypeStruct((1, 128), F32),
        ),
        in_specs=[hbm] * 6,
        out_specs=(pl.BlockSpec(memory_space=pl.ANY), vmem, vmem),
        scratch_shapes=[
            pltpu.VMEM((NCORE, rows, width), BF16),
            pltpu.VMEM(block, BF16),
            pltpu.VMEM(block, BF16),
            pltpu.VMEM((NCORE, rows, tokens), BF16),
            pltpu.VMEM((1, 128), jnp.int32),
            pltpu.VMEM((1, 128), jnp.int32),
            pltpu.VMEM((16, 128), BF16),
            pltpu.VMEM((NLO, NCORE, 16, 128), BF16),
            pltpu.VMEM((2, 16, 896), F32),
            pltpu.VMEM((NX, 2, NHI, NY, 16, 896), BF16),
            pltpu.VMEM((NXY, 4, 128), F32),
            pltpu.VMEM((NZ, 4, 128), F32),
            pltpu.VMEM((NCORE, rows, tokens), F32),
            pltpu.VMEM((NCORE, rows, tokens), F32),
            pltpu.VMEM((NX, NY, 2, 16, 896), BF16),
            pltpu.VMEM((NXY, 2, 16, 896), BF16),
            pltpu.VMEM((128, 128), F32),
            pltpu.VMEM((NLO, NCORE, 8, 128), F32),
            pltpu.VMEM((NZ, 8, 128), F32),
            pltpu.VMEM((rows, tokens), BF16),
            pltpu.VMEM((NCORE, rows, tokens), BF16),
            pltpu.VMEM((NCORE, 8, 128), F32),
            pltpu.VMEM((rows, width), BF16),
            dma((6,)),
            dma,
            dma((2,)),
            dma((2, 2)),
            dma((2,)),
            dma((2, NXY)),
            dma((2, 2)),
            dma((2, 2)),
            dma((2,)),
            dma((2,)),
            dma((2, 2)),
        ],
        compiler_params=pltpu.CompilerParams(
            collective_id=0, has_side_effects=True, vmem_limit_bytes=VMEM_MIB * 1024 * 1024
        ),
    )(
        table,
        hidden_states,
        embed_cotangent,
        teacher_logits,
        student_ids.reshape(1, 128),
        loss_mask.reshape(1, 128),
    )
    results = (table_grad, state_grad, loss)
    table_grad, state_grad, loss = pl.pallas_call(
        hand_over,
        out_shape=[jax.ShapeDtypeStruct(r.shape, r.dtype) for r in results],
        in_specs=[pl.BlockSpec(memory_space=pl.ANY)] * 3,
        out_specs=[pl.BlockSpec(memory_space=pl.ANY)] * 3,
        scratch_shapes=[*(pltpu.VMEM(r.shape, r.dtype) for r in results), dma((NX + 2,)), dma((NX + 2,))],
        compiler_params=pltpu.CompilerParams(vmem_limit_bytes=VMEM_MIB * 1024 * 1024),
    )(*results)
    return table_grad, state_grad, loss[0, 0]


def solution(mesh):
    return jax.shard_map(
        shards,
        mesh=mesh,
        in_specs=(
            P(("section", "fsdp"), None),
            P("fsdp", "section"),
            P("fsdp", "section"),
            P(("section", "fsdp"), None),
            P(),
            P(),
        ),
        out_specs=(P(("section", "fsdp"), None), P("fsdp", "section"), P()),
        check_vma=False,
    )
```

```python
import functools

import jax
import jax.numpy as jnp
from jax import lax
from jax.experimental import pallas as pl
from jax.experimental.pallas import tpu as pltpu
from jax.sharding import PartitionSpec as P

MESH = pl.DeviceIdType.MESH
F32, BF16 = jnp.float32, jnp.bfloat16
CONTRACT_LAST = (((1,), (1,)), ((), ()))
CONTRACT_FIRST = (((0,), (0,)), ((), ()))
NX, NY, NLO, NHI, NCORE = 4, 4, 8, 2, 2
NZ = NLO * NHI
NXY = NX * NY
VMEM_MIB = 60
FAR_Z = sorted(range(1, NZ), key=lambda j: -min(j, NZ - j))
FAR_XY = sorted(
    ((i, j) for i in range(NX) for j in range(NY) if i or j), key=lambda d: -sum(min(v, 4 - v) for v in d)
)


def merge(maxes, *sums):
    top = jnp.max(maxes, axis=0, keepdims=True)
    scale = jnp.exp(maxes - top)
    return (top, *(jnp.sum(s * scale, axis=0, keepdims=True) for s in sums))


def merge_tiles(ref):
    return merge(ref[:, 0, :], ref[:, 1, :], ref[:, 2, :])


def tile_of(rows):
    return jnp.concatenate([*rows, jnp.zeros((1, 128), F32)], axis=0)


class Copies:
    def __init__(self):
        self.arrivals, self.departures = {}, {}

    @staticmethod
    def wait(ref, sem):
        pltpu.make_async_copy(ref, ref, sem).wait()

    @staticmethod
    def send(src, dst, sems, target):
        pltpu.make_async_remote_copy(
            src_ref=src, dst_ref=dst, send_sem=sems[0], recv_sem=sems[1], device_id=target, device_id_type=MESH
        ).start()

    def expect(self, key, ref, sems):
        self.arrivals[key] = (ref, sems[1])
        self.departures[key] = (ref, sems[0])

    def arrive(self, key):
        self.wait(*self.arrivals.pop(key))

    def finish(self):
        for key in list(self.arrivals):
            self.arrive(key)
        for ref, sem in self.departures.values():
            self.wait(ref, sem)


def kernel(
    table_hbm, hidden_hbm, cot_hbm, teach_hbm, ids_hbm, mask_hbm,
    grad_hbm, state_ref, loss_ref,
    table, hidden_in, cot_in, teach_in, ids_in, mask_in,
    pack, first, lanes, hc, stat_xy, stat_z, teach_ref, logits_ref,
    t_ref, u_ref, cols_ref, z_src, z_dst, g_out, g_all, loss_x, grad_ref,
    load_sem, store_sem, ag1_sem, pre_sem, plane_send, plane_recv, sib_sem, st_sem, rs1_sem, rs2_sem, g_sem,
):
    section, fsdp = lax.axis_index("section"), lax.axis_index("fsdp")
    x, lo = section // NLO, lax.rem(section, NLO)
    y, hi, core = fsdp // (NHI * NCORE), lax.rem(fsdp // NCORE, NHI), lax.rem(fsdp, NCORE)
    z, me = hi * NLO + lo, x * NY + y
    other = 1 - core

    def device(x_, y_, z_, core_):
        return (x_ * NLO + lax.rem(z_, NLO), y_ * (NHI * NCORE) + (z_ // NLO) * NCORE + core_)

    sibling = device(x, y, z, other)
    along_z = [lax.rem(z + j, NZ) for j in FAR_Z]
    in_plane = [(lax.rem(x + i, NX), lax.rem(y + j, NY)) for i, j in FAR_XY]
    copies = Copies()
    send = copies.send

    def pair(ref, *at):
        return ref.at[(0, *at)], ref.at[(1, *at)]

    def own_half(v):
        halves = [
            jnp.concatenate([v[:, 32 * q + 16 * h : 32 * q + 16 * h + 16] for q in range(NY)] * 2, axis=1)
            for h in range(2)
        ]
        return jnp.where(core == 0, halves[0], halves[1])

    def left_lanes(shape):
        return lax.broadcasted_iota(jnp.int32, shape, 1) < 64

    loads = [
        pltpu.make_async_copy(src, dst, load_sem.at[i])
        for i, (src, dst) in enumerate(
            [
                (hidden_hbm, hidden_in), (cot_hbm, cot_in), (teach_hbm, teach_in.at[core]),
                (table_hbm, table.at[core]), (ids_hbm, ids_in), (mask_hbm, mask_in),
            ]
        )
    ]
    loads[0].start()
    loads[1].start()

    barrier = pltpu.get_barrier_semaphore()
    for z_ in along_z:
        pl.semaphore_signal(barrier, inc=1, device_id=device(x, y, z_, core), device_id_type=MESH)
        pl.semaphore_signal(barrier, inc=1, device_id=device(x, y, z_, other), device_id_type=MESH)
    for x_, y_ in in_plane:
        pl.semaphore_signal(barrier, inc=1, device_id=device(x_, y_, z, core), device_id_type=MESH)
    pl.semaphore_signal(barrier, inc=1, device_id=sibling, device_id_type=MESH)
    for load in loads[2:]:
        load.start()

    loads[0].wait()
    loads[1].wait()
    pack[...] = jnp.zeros_like(pack)
    pack[:, 0:112] = jnp.concatenate([hidden_in[...].astype(F32), cot_in[...].astype(F32)], axis=0).astype(BF16)
    pl.semaphore_wait(barrier, 1 + 2 * (NZ - 1) + NXY - 1)

    sems = pair(ag1_sem)
    for z_ in along_z:
        send(pack, first.at[lo, core], sems, device(x, y, z_, hi))

    @pl.when(core == hi)
    def _():
        pltpu.make_async_copy(pack, first.at[lo, core], sems[1]).start()

    @pl.when(core != hi)
    def _():
        send(pack, first.at[lo, core], sems, device(x, y, z, hi))

    for i, (src, dst) in enumerate(((teach_hbm, teach_in), (table_hbm, table))):
        sems = pair(pre_sem, i)
        send(src, dst.at[core], sems, sibling)
        copies.expect(("pre", i), dst.at[0], sems)
    for load in loads[2:]:
        load.wait()
    copies.arrive(("pre", 0))
    for s in range(2):
        teach_ref[s] = own_half(teach_in[s].astype(F32))
    top_t = jnp.max(jnp.maximum(teach_ref[0], teach_ref[1]), axis=0, keepdims=True)
    total_t = jnp.sum(jnp.exp(teach_ref[0] - top_t) + jnp.exp(teach_ref[1] - top_t), axis=0, keepdims=True)
    weight = own_half(mask_in[...].astype(F32) / 128.0)

    copies.wait(first, ag1_sem.at[1])

    def share(t):
        block = hc.at[x, t, core, y]
        for x_, y_ in in_plane:
            send(block, block, (plane_send.at[t], plane_recv.at[t, me]), device(x_, y_, z, core))

    def gathered(t):
        for x_, y_ in in_plane[::-1]:
            copies.wait(hc.at[x_, t, core, y_], plane_recv.at[t, x_ * NY + y_])

    def to_sibling(t):
        half = hc.at[:, t, core]
        send(half, half, pair(sib_sem, t), sibling)
        copies.expect(("sib", t), half, pair(sib_sem, t))

    for t in range(2):
        for j in range(NLO):
            left, right = first[j, 0].astype(F32), first[j, 1].astype(F32)
            rows = jnp.concatenate([left[8 * t : 8 * t + 8], right[8 * t : 8 * t + 8]], axis=0)
            lanes[t, :, 112 * j : 112 * (j + 1)] = rows[:, 0:112]
        hc[x, t, core, y] = lanes[t].astype(BF16)
        if t == 0:
            share(0)
    copies.arrive(("pre", 1))
    total = [None, None]
    for i in (0, 1, 3, 2):
        c = lax.rem(x + i, NX)
        for j in (0, 1, 3, 2):
            if i or j:
                y_ = lax.rem(y + j, NY)
                copies.wait(hc.at[c, 0, core, y_], plane_recv.at[0, c * NY + y_])
        states = hc[c, 0, core].reshape(64, 896)
        states = jnp.concatenate([states, states], axis=0)
        at = pl.ds(pl.multiple_of(896 * c, 128), 896)
        for s in range(2):
            term = lax.dot_general(table[s, :, at], states, CONTRACT_LAST, preferred_element_type=F32)
            total[s] = term if i == 0 else total[s] + term
    peak = jnp.max(jnp.maximum(total[0], total[1]), axis=0, keepdims=True)
    p = [jnp.exp(t - peak) for t in total]
    gap = [t - teach_ref[s] for s, t in enumerate(total)]
    chip_sum = jnp.sum(p[0] + p[1], axis=0, keepdims=True)
    chip_cross = jnp.sum(p[0] * gap[0] + p[1] * gap[1], axis=0, keepdims=True)
    left = left_lanes(peak.shape)
    stat_xy[me] = tile_of([jnp.where(left, peak, top_t), jnp.where(left, chip_sum, total_t), jnp.where(left, chip_cross, 0.0)])
    sems = pair(st_sem, 0)
    for x_, y_ in in_plane:
        send(stat_xy.at[me], stat_xy.at[me], sems, device(x_, y_, z, core))
    copies.expect("st1", stat_xy.at[0 : NXY - 1], sems)
    logits_ref[0] = total[0]
    logits_ref[1] = total[1]

    mean = chip_cross / chip_sum
    both = [
        jnp.where(left_lanes(p[s].shape), p[s] * (gap[s] - mean), p[s]).astype(BF16) for s in range(2)
    ]
    sems = pair(rs1_sem)
    for i, c in enumerate([lax.rem(x + i, NX) for i in (2, 1, 3, 0)]):
        at = pl.ds(pl.multiple_of(896 * c, 128), 896)
        sums = lax.dot_general(both[0], table[0, :, at], CONTRACT_FIRST, preferred_element_type=F32)
        sums = sums + lax.dot_general(both[1], table[1, :, at], CONTRACT_FIRST, preferred_element_type=F32)
        sums = sums.astype(BF16).reshape(2, NY, 16, 896)
        for r in range(NY):
            for k in range(2):
                t_ref[i, r, k] = sums[k, r]
        for j in (2, 1, 3, 0):
            y_ = lax.rem(y + j, NY)
            if i < 3 or j > 0:
                send(t_ref.at[i, y_], u_ref.at[me], sems, device(c, y_, z, core))
            else:
                u_ref[me] = t_ref[i, y_]
    copies.expect("rs1", u_ref.at[0 : NXY - 1], sems)

    copies.arrive("st1")
    stat_z[z] = tile_of(merge_tiles(stat_xy))
    sems = pair(st_sem, 1)
    for z_ in along_z:
        send(stat_z.at[z], stat_z.at[z], sems, device(x, y, z_, core))
    copies.expect("st2", stat_z.at[0 : NZ - 1], sems)
    share(1)
    to_sibling(0)
    z_src[...] = jnp.zeros_like(z_src)
    means = stat_xy[:, 2, :] / stat_xy[:, 1, :]
    copies.arrive("st2")
    merged = merge_tiles(stat_z)
    swapped = [jnp.concatenate([v[:, 64:128], v[:, 0:64]], axis=1) for v in merged]
    peak_s, sum_s, cross = (jnp.where(left, v, w) for v, w in zip(merged, swapped, strict=True))
    peak_t, sum_t = (jnp.where(left, w, v) for v, w in zip(merged[:2], swapped[:2], strict=True))

    scale = weight / sum_s * jnp.exp(stat_xy[:, 0, :] - peak_s)
    shift = scale * (means - cross / sum_s)
    cols_ref[...] = jnp.concatenate([scale, shift, jnp.zeros((128 - 2 * NXY, 128), F32)], axis=0).T
    cols = cols_ref[pl.ds(pl.multiple_of(y * 16, 16), 16), :]

    copies.arrive("rs1")
    acc = jnp.zeros((16, 896), F32)
    for j in range(NXY):
        acc = acc + cols[:, j : j + 1] * u_ref[j, 0].astype(F32)
        acc = acc + cols[:, NXY + j : NXY + j + 1] * u_ref[j, 1].astype(F32)
    lanes[0] = acc
    for j in range(NLO):
        for k in range(NCORE):
            z_src[j, k, :, 0:112] = lanes[0, 8 * k : 8 * k + 8, 112 * j : 112 * (j + 1)]

    sems = pair(rs2_sem)
    for j in (0, 7, 1, 6, 2, 5, 3, 4):
        lo_ = lax.rem(lo + j, NLO)
        send(z_src.at[lo_, other], z_dst.at[z], sems, device(x, y, core * NLO + lo_, other))
        if j > 0:
            send(z_src.at[lo_, core], z_dst.at[z], sems, device(x, y, core * NLO + lo_, core))
        else:

            @pl.when(core == hi)
            def _():
                pltpu.make_async_copy(z_src.at[lo, core], z_dst.at[z], sems[1]).start()

            @pl.when(core != hi)
            def _():
                send(z_src.at[lo, core], z_dst.at[z], sems, device(x, y, core * NLO + lo, core))

    log_zs = peak_s + jnp.log(sum_s)
    log_zt = peak_t + jnp.log(sum_t)
    kl_term = cross / sum_s - log_zs + log_zt
    part = jnp.sum(jnp.where(left_lanes(weight.shape), weight * kl_term, 0.0), axis=1, keepdims=True)

    def logits_grad(s):
        logits = logits_ref[s]
        inner = jnp.exp(logits - log_zs) * (logits - teach_ref[s] - log_zs + log_zt - kl_term)
        return (weight * inner).astype(BF16)

    loss_x[core] = jnp.broadcast_to(part, (8, 128))
    g_out[...] = logits_grad(other)
    for i, (src, dst) in enumerate(((g_out, g_all.at[core]), (loss_x.at[core], loss_x.at[core]))):
        send(src, dst, pair(g_sem, i), sibling)
        copies.expect(("g", i), dst, pair(g_sem, i))
    own = logits_grad(core)
    gathered(1)
    to_sibling(1)
    ids = ids_in[...]
    ids = jnp.concatenate([ids[:, 32 * q + 16 * h : 32 * q + 16 * h + 16] for h in range(2) for q in range(NY)], axis=1)
    rows = own.shape[0]
    entries = (section * (NY * NHI * NCORE) + fsdp) * rows + lax.broadcasted_iota(jnp.int32, (rows, 128), 0)
    selector = (entries == ids).astype(BF16)
    for i in range(2):
        copies.arrive(("g", i))
    for t in range(2):
        copies.arrive(("sib", t))
    loss_ref[...] = loss_x[0, 0:1] + loss_x[1, 0:1]
    mine = left_lanes(own.shape) == (core == 0)
    glog = jnp.where(mine, own.astype(F32), g_all[other].astype(F32)).astype(BF16)
    both = jnp.concatenate([glog, selector], axis=1)
    for c in range(NX):
        grad_ref[:, 896 * c : 896 * (c + 1)] = jnp.dot(
            both, hc[c].reshape(256, 896), preferred_element_type=F32
        ).astype(BF16)
    store = pltpu.make_async_copy(grad_ref, grad_hbm, store_sem)
    store.start()
    copies.wait(z_dst, rs2_sem.at[1])
    state_ref[...] = jnp.sum(z_dst[...], axis=0)[:, 0:112].astype(BF16)

    tiles = first.reshape(NZ, 16, 128)

    @pl.when(core == hi)
    def _():
        copies.wait(tiles.at[0 : NZ - 1], ag1_sem.at[0])
        copies.wait(z_dst.at[0 : NZ - 1], rs2_sem.at[0])

    @pl.when(core != hi)
    def _():
        copies.wait(tiles, ag1_sem.at[0])
        copies.wait(z_dst, rs2_sem.at[0])

    for t in range(2):
        copies.wait(hc.at[0:3, t, 0, 0:4], plane_send.at[t])
        copies.wait(hc.at[0:3, t, 0, 0], plane_send.at[t])
    copies.finish()
    store.wait()


def hand_over(grad, state, loss, grad_out, state_out, loss_out, grad_v, state_v, loss_v, in_sem, out_sem):
    parts = [(grad.at[:, at], grad_v.at[:, at], grad_out.at[:, at]) for at in (pl.ds(896 * c, 896) for c in range(NX))]
    parts = [(state, state_v, state_out), (loss, loss_v, loss_out), *parts]
    loads = [pltpu.make_async_copy(src, via, in_sem.at[i]) for i, (src, via, _) in enumerate(parts)]
    stores = [pltpu.make_async_copy(via, dst, out_sem.at[i]) for i, (_, via, dst) in enumerate(parts)]
    for load in loads:
        load.start()
    for load, store in zip(loads, stores):
        load.wait()
        store.start()
    for store in stores:
        store.wait()


def shards(table, hidden_states, embed_cotangent, teacher_logits, student_ids, loss_mask):
    rows, width = table.shape
    tokens = teacher_logits.shape[1]
    block = hidden_states.shape
    vmem = pl.BlockSpec(memory_space=pltpu.VMEM)
    hbm = pl.BlockSpec(memory_space=pltpu.HBM)
    dma = pltpu.SemaphoreType.DMA
    table_grad, state_grad, loss = pl.pallas_call(
        kernel,
        out_shape=(
            jax.ShapeDtypeStruct((rows, width), BF16),
            jax.ShapeDtypeStruct(block, BF16),
            jax.ShapeDtypeStruct((1, 128), F32),
        ),
        in_specs=[hbm] * 6,
        out_specs=(pl.BlockSpec(memory_space=pl.ANY), vmem, vmem),
        scratch_shapes=[
            pltpu.VMEM((NCORE, rows, width), BF16),
            pltpu.VMEM(block, BF16),
            pltpu.VMEM(block, BF16),
            pltpu.VMEM((NCORE, rows, tokens), BF16),
            pltpu.VMEM((1, 128), jnp.int32),
            pltpu.VMEM((1, 128), jnp.int32),
            pltpu.VMEM((16, 128), BF16),
            pltpu.VMEM((NLO, NCORE, 16, 128), BF16),
            pltpu.VMEM((2, 16, 896), F32),
            pltpu.VMEM((NX, 2, NHI, NY, 16, 896), BF16),
            pltpu.VMEM((NXY, 4, 128), F32),
            pltpu.VMEM((NZ, 4, 128), F32),
            pltpu.VMEM((NCORE, rows, tokens), F32),
            pltpu.VMEM((NCORE, rows, tokens), F32),
            pltpu.VMEM((NX, NY, 2, 16, 896), BF16),
            pltpu.VMEM((NXY, 2, 16, 896), BF16),
            pltpu.VMEM((128, 128), F32),
            pltpu.VMEM((NLO, NCORE, 8, 128), F32),
            pltpu.VMEM((NZ, 8, 128), F32),
            pltpu.VMEM((rows, tokens), BF16),
            pltpu.VMEM((NCORE, rows, tokens), BF16),
            pltpu.VMEM((NCORE, 8, 128), F32),
            pltpu.VMEM((rows, width), BF16),
            dma((6,)),
            dma,
            dma((2,)),
            dma((2, 2)),
            dma((2,)),
            dma((2, NXY)),
            dma((2, 2)),
            dma((2, 2)),
            dma((2,)),
            dma((2,)),
            dma((2, 2)),
        ],
        compiler_params=pltpu.CompilerParams(
            collective_id=0, has_side_effects=True, vmem_limit_bytes=VMEM_MIB * 1024 * 1024
        ),
    )(
        table,
        hidden_states,
        embed_cotangent,
        teacher_logits,
        student_ids.reshape(1, 128),
        loss_mask.reshape(1, 128),
    )
    results = (table_grad, state_grad, loss)
    table_grad, state_grad, loss = pl.pallas_call(
        hand_over,
        out_shape=[jax.ShapeDtypeStruct(r.shape, r.dtype) for r in results],
        in_specs=[pl.BlockSpec(memory_space=pl.ANY)] * 3,
        out_specs=[pl.BlockSpec(memory_space=pl.ANY)] * 3,
        scratch_shapes=[*(pltpu.VMEM(r.shape, r.dtype) for r in results), dma((NX + 2,)), dma((NX + 2,))],
        compiler_params=pltpu.CompilerParams(vmem_limit_bytes=VMEM_MIB * 1024 * 1024),
    )(*results)
    return table_grad, state_grad, loss[0, 0]


def solution(mesh):
    return jax.shard_map(
        shards,
        mesh=mesh,
        in_specs=(
            P(("section", "fsdp"), None),
            P("fsdp", "section"),
            P("fsdp", "section"),
            P(("section", "fsdp"), None),
            P(),
            P(),
        ),
        out_specs=(P(("section", "fsdp"), None), P("fsdp", "section"), P()),
        check_vma=False,
    )
```
